256 devices in a mesh: seq: 32 (over y, z), tp: 8 (over x, core).
Axes of the slice: x: 4, y: 4, z: 8, core: 2. Of those that a mesh axis runs over, the one named last changes fastest.
Arguments:
- decode_query: bfloat16 [4, 8192], P(None, 'tp'), may hold values from -180 to 180, as said below
- cache_keys: bfloat16 [4, 65536, 1024], P(None, 'seq', 'tp'), may hold values from -6 to 6
- cache_values: bfloat16 [4, 65536, 1024], P(None, 'seq', 'tp'), may hold values from -6 to 6
- cache_len: int32 [4], replicated, may hold values from 2048 to 65536, as said below
- prefill_rows: bfloat16 [1024, 8192], P(None, 'seq'), may hold values from -8 to 8
- key_weight: bfloat16 [8192, 1024], P('seq', 'tp'), may hold values from -0.0625 to 0.0625
- value_weight: bfloat16 [8192, 1024], P('seq', 'tp'), may hold values from -0.0625 to 0.0625
- span_request: int32 [1024], replicated, may hold values from 0 to 3
- span_target: int32 [1024, 1], replicated, may hold values from 0 to 31; in each aligned block of 32 rows (0 to 31, 32 to 63, ...) at most 2 rows name the same one
- out_weight: bfloat16 [8192, 8192], P('tp', 'seq'), may hold values from -0.1875 to 0.1875
Outputs:
- layer_out: bfloat16 [4, 8192], P(None, 'seq')
- appended_keys: bfloat16 [2048, 1024], P('seq', 'tp')
- appended_values: bfloat16 [2048, 1024], P('seq', 'tp')
The draws below stay inside these ranges and needn't reach their ends.
Inputs may be any that keep to these rules, and one draw needn't show every extreme that they name: `cache_len`: some request has all 65536 positions live. `decode_query`: in the hidden draw some queries are large multiples of cached keys. `span_target`: among the 32 tokens owned by one index of seq, at most 2 share a target, and 2 do in some owners.
All inputs are finite; a program needn't handle non-finite values.
Results may differ from the reference program's by a relative error of at most 0.03.
Values may be sent and summed in bfloat16 or wider, within the bound.
No kernel may reach another device: no remote copies, remote signals or barrier semaphores. Data moves between devices by JAX's collectives and lax.ppermute only.
A program may use at most 64 MiB of HBM per device.

```python
import math
import jax
import jax.numpy as jnp
import numpy as np
from jax import lax

D = 8192
H = 64
KVH = 8
HD = 128
R = 4
L_DEV = 2048
PRE_DEV = 32
CAP = 2
LTOT = 65536
PRE = 1024
N_SEQ = 32


def draw_cache_keys(key, part):
    key = jax.random.fold_in(key, 11)
    key_rows = jnp.clip(jax.random.normal(key, (R, LTOT, KVH * HD), jnp.float32), -6.0, 6.0)
    return key_rows.astype(jnp.bfloat16)


def draw_decode_query(key, part):
    key = jax.random.fold_in(key, 13)
    query_rows = 3.0 * jnp.clip(jax.random.normal(key, (R, H * HD), jnp.float32), -6.0, 6.0)
    return query_rows.astype(jnp.bfloat16)


def draw_cache_len(key, part):
    key = jax.random.fold_in(key, 17)
    lengths = jax.random.randint(key, (R,), L_DEV, LTOT + 1)
    longest = jax.random.randint(jax.random.fold_in(key, 1), (), 0, R)
    return jnp.where(jnp.arange(R) == longest, LTOT, lengths).astype(jnp.int32)


def plant(values, own_key, smallest, largest):
    spot = [jax.random.randint(jax.random.fold_in(own_key, axis), (), 0, length) for axis, length in enumerate(values.shape)]
    widest = values.shape.index(max(values.shape))
    next_to = spot[:widest] + [(spot[widest] + 1) % values.shape[widest]] + spot[widest + 1:]
    return values.at[tuple(spot)].set(smallest).at[tuple(next_to)].set(largest)


def block_levels(key, dims, cuts, least, largest):
    level = 1.0
    for position, parts in cuts:
        draws = jax.random.uniform(jax.random.fold_in(jax.random.fold_in(key, 6), position), (parts,), jnp.float32, least / len(cuts), largest / len(cuts))
        level = level * jnp.repeat(jnp.exp(draws), dims[position] // parts).reshape((-1,) + (1,) * (len(dims) - 1 - position))
    return level


def deal_out(rng, own, number, rows, count, top, limit, skew):
    sequence = jax.random.permutation(rng, count)
    packed, usual = portions_of(count, rows * top, limit, skew, True), portions_of(count, rows * top, limit, skew, False)
    places = jnp.arange(count)

    def named(sizes, turn):
        used = int((sizes > 0).sum())
        fixed = max(1, used // 4)
        moved = fixed + (places - fixed + turn * (used - fixed)) % max(1, count - fixed)
        return jnp.zeros((count,), jnp.int32).at[sequence[jnp.where(places < fixed, places, moved)]].set(jnp.asarray(sizes, jnp.int32))

    sizes = jnp.where(number % 4 == 0, named(packed, number // 4), named(usual, number - number // 4 - 1))
    mixed = jax.random.permutation(jax.random.fold_in(own, 3), count)
    source_of, sink = mixed[0:count // 2 * 2:2], mixed[1:count // 2 * 2:2]
    margin = jnp.minimum(sizes[source_of] - 1, limit - sizes[sink]) // 2
    margin = jnp.where((source_of == sequence[0]) | (sink == sequence[0]) | (sizes[sink] == 0), 0, jnp.maximum(margin, 0))
    moved = jax.random.randint(jax.random.fold_in(own, 4), (count // 2,), 0, 1 << 20) % (margin + 1)
    sizes = sizes.at[source_of].add(-moved).at[sink].add(moved)
    items = jnp.searchsorted(jnp.cumsum(sizes), jnp.arange(rows * top), side="right").astype(jnp.int32)
    listing = items.reshape(top, rows).T
    listing = listing[jax.random.permutation(jax.random.fold_in(own, 1), rows)]
    turn = jax.random.randint(jax.random.fold_in(own, 2), (rows, 1), 0, top)
    return jnp.take_along_axis(listing, (jnp.arange(top)[None, :] + turn) % top, axis=1)


def portions_of(count, total, reach, slope, full):
    portions = [(1 << 20) // math.isqrt(grade ** slope) + 1 for grade in range(1, count + 1)]
    largest = reach if full else min(reach, max(-(-total // count), total * portions[0] // sum(portions)))
    least = 1 if total - largest >= count - 1 else 0
    holding, spare = [largest] + [least] * (count - 1), total - largest - least * (count - 1)
    while spare > 0:
        free = [i for i in range(1, count) if holding[i] < largest] or [i for i in range(1, count) if holding[i] < reach]
        pool, left = sum([portions[i] for i in free]), spare
        for i in free:
            extra = min(reach - holding[i], max(1, left * portions[i] // pool), spare)
            holding[i] = holding[i] + extra
            spare = spare - extra
    return np.array(holding)


def gaussian(rng, extent, scale, reach, split=(), dtype=jnp.bfloat16):
    result = scale * jax.random.normal(rng, extent, jnp.float32)
    if split:
        result = result * block_levels(rng, extent, split, -0.22, 0.18)
    return jnp.clip(result, -reach, reach).astype(dtype)


def setup_inputs(seed: int = 0) -> dict:
    arg_keys = jax.random.split(jax.random.key(seed), 11)
    decode_query = draw_decode_query(jax.random.fold_in(arg_keys[10], 71), 0)
    cache_keys = draw_cache_keys(jax.random.fold_in(arg_keys[10], 71), 0)
    cache_values = gaussian(arg_keys[2], (R, LTOT, KVH * HD), 1.0, 6.0, ((1, 32), (2, 8)))
    cache_len = draw_cache_len(jax.random.fold_in(arg_keys[10], 71), 0)
    prefill_rows = gaussian(arg_keys[4], (PRE, D), 1.6, 8.0, ((1, 32),))
    key_weight = gaussian(arg_keys[5], (D, KVH * HD), D ** -0.5, 0.0625, ((0, 32), (1, 8)))
    value_weight = gaussian(arg_keys[6], (D, KVH * HD), D ** -0.5, 0.0625, ((0, 32), (1, 8)))
    span_request = plant(jax.random.randint(arg_keys[7], (PRE,), 0, R), jax.random.fold_in(arg_keys[7], 1), 0, R - 1).astype(jnp.int32)
    span_target_keys = jax.random.split(jax.random.fold_in(arg_keys[8], 1), PRE // PRE_DEV)
    span_target_turns = jax.random.permutation(jax.random.fold_in(arg_keys[8], 3), PRE // PRE_DEV)
    span_target = jax.vmap(lambda own, number: deal_out(jax.random.fold_in(arg_keys[8], 2), own, number, PRE_DEV, N_SEQ, 1, CAP, 2))(span_target_keys, span_target_turns).reshape((PRE, 1))
    out_weight = gaussian(arg_keys[9], (H * HD, D), (HD * H // KVH) ** -0.5, 0.1875, ((0, 8), (1, 32)))
    return {"decode_query": decode_query, "cache_keys": cache_keys, "cache_values": cache_values, "cache_len": cache_len, "prefill_rows": prefill_rows, "key_weight": key_weight, "value_weight": value_weight, "span_request": span_request, "span_target": span_target, "out_weight": out_weight}


def reference(decode_query, cache_keys, cache_values, cache_len, prefill_rows, key_weight, value_weight, span_request, span_target, out_weight):
    span_keys = jnp.dot(prefill_rows, key_weight, preferred_element_type=jnp.float32).astype(jnp.bfloat16)
    span_values = jnp.dot(prefill_rows, value_weight, preferred_element_type=jnp.float32).astype(jnp.bfloat16)
    targets = span_target[:, 0].astype(jnp.int32)
    blocks = targets.reshape(N_SEQ, PRE_DEV)
    positions = jnp.arange(PRE_DEV)
    earlier = positions[None, :] < positions[:, None]
    slot_rank = lax.optimization_barrier(jnp.sum((blocks[:, :, None] == blocks[:, None, :]) & earlier[None], axis=2)).astype(jnp.int32).reshape(-1)
    sources = (jnp.arange(PRE) // PRE_DEV).astype(jnp.int32)
    slot_index = targets * (N_SEQ * CAP) + sources * CAP + slot_rank
    appended_keys = jnp.zeros((N_SEQ * N_SEQ * CAP, KVH * HD), jnp.bfloat16).at[slot_index].set(span_keys)
    appended_values = jnp.zeros((N_SEQ * N_SEQ * CAP, KVH * HD), jnp.bfloat16).at[slot_index].set(span_values)
    score_scale = 1.0 / math.sqrt(HD)
    per_group = H // KVH
    outputs = []
    for request in range(R):
        query_rows = decode_query[request].astype(jnp.float32).reshape(KVH, per_group, HD)
        live_keys = jnp.concatenate([jnp.arange(LTOT) < cache_len[request], span_request == request])
        head_rows = []
        for kv_group in range(KVH):
            low = kv_group * HD
            key_rows = jnp.concatenate([cache_keys[request, :, low:low + HD], span_keys[:, low:low + HD]]).astype(jnp.float32)
            value_rows = jnp.concatenate([cache_values[request, :, low:low + HD], span_values[:, low:low + HD]])
            scores = jnp.dot(query_rows[kv_group], key_rows.T, precision=lax.Precision.HIGHEST) * score_scale
            scores = jnp.where(live_keys[None, :], scores, -1e+30)
            row_top = lax.optimization_barrier(jnp.max(scores, axis=1, keepdims=True))
            weights = jnp.where(live_keys[None, :], jnp.exp(scores - row_top), 0.0)
            rounded_weights = weights.astype(jnp.bfloat16)
            weighted = jnp.dot(rounded_weights, value_rows, preferred_element_type=jnp.float32)
            head_rows.append(weighted / lax.optimization_barrier(jnp.sum(weights, axis=1, keepdims=True)))
        outputs.append(jnp.concatenate(head_rows, axis=0).reshape(-1))
    attended = jnp.stack(outputs).astype(jnp.bfloat16)
    layer_out = jnp.dot(attended, out_weight, preferred_element_type=jnp.float32).astype(jnp.bfloat16)
    return (layer_out, appended_keys, appended_values)
```

```python
import functools

import jax
import jax.numpy as jnp
from jax import lax
from jax.experimental import pallas as pl
from jax.experimental.pallas import tpu as pltpu
from jax.sharding import PartitionSpec as P

H = 64
KVH = 8
HD = 128
CAP = 2
DEAD = -(2.0**100)
TAIL = 8
VMEM = pltpu.VMEM
SMEM = pltpu.SMEM


def whole(space=VMEM):
    return pl.BlockSpec(memory_space=space)


def project_kernel(rows_ref, key_ref, value_ref, out_ref):
    rows = rows_ref[...]
    out_ref[:, :HD] = jnp.dot(
        rows, key_ref[...], preferred_element_type=jnp.float32
    ).astype(jnp.bfloat16)
    out_ref[:, HD:] = jnp.dot(
        rows, value_ref[...], preferred_element_type=jnp.float32
    ).astype(jnp.bfloat16)


def project(rows, key_weight, value_weight):
    tokens, features = rows.shape
    steps = 4
    return pl.pallas_call(
        project_kernel,
        grid=(steps,),
        in_specs=[
            pl.BlockSpec((tokens // steps, features), lambda i: (i, 0)),
            pl.BlockSpec((features, HD), lambda i: (0, 0)),
            pl.BlockSpec((features, HD), lambda i: (0, 0)),
        ],
        out_specs=pl.BlockSpec((tokens // steps, 2 * HD), lambda i: (i, 0)),
        out_shape=jax.ShapeDtypeStruct((tokens, 2 * HD), jnp.bfloat16),
        name="project",
    )(rows, key_weight, value_weight)


def stacked_queries(query_ref, per_group):
    query = query_ref[...]
    return jnp.concatenate(
        [query[:, h * HD : (h + 1) * HD] for h in range(per_group)], axis=0
    )


def cache_kernel(
    requests,
    per_group,
    len_ref,
    query_ref,
    keys_ref,
    values_ref,
    target_ref,
    request_ref,
    o_ref,
    m_ref,
    l_ref,
    place_key_ref,
    place_value_ref,
    live_ref,
):
    request = pl.program_id(0)
    seq_index = lax.axis_index("seq")
    rows = requests * per_group
    local_len = keys_ref.shape[1]

    @pl.when(request == 0)
    def _():
        o_ref[...] = jnp.zeros_like(o_ref)
        l_ref[...] = jnp.zeros_like(l_ref)
        m_ref[...] = jnp.full(m_ref.shape, DEAD, jnp.float32)
        tokens = target_ref.shape[1]
        target = jnp.broadcast_to(target_ref[pl.ds(seq_index, 1), :], (tokens, tokens))
        i = lax.broadcasted_iota(jnp.int32, (tokens, tokens), 0)
        j = lax.broadcasted_iota(jnp.int32, (tokens, tokens), 1)
        column = jnp.sum(jnp.where(i == j, target, 0), axis=1, keepdims=True)
        rank = jnp.sum(
            jnp.where((column == target) & (i < j), 1, 0), axis=0, keepdims=True
        )
        slot = target[0:1, :] * CAP + rank
        count = place_key_ref.shape[0]
        row = lax.broadcasted_iota(jnp.int32, (count, tokens), 0)
        dest, within = row // TAIL, row % TAIL
        wanted = jnp.broadcast_to(slot, (count, tokens))
        is_key = (within < CAP) & (wanted == dest * CAP + within)
        is_value = (within >= CAP) & (within < 2 * CAP) & (wanted == dest * CAP + within - CAP)
        place_key_ref[...] = jnp.where(is_key, 1.0, 0.0).astype(jnp.bfloat16)
        place_value_ref[...] = jnp.where(is_value, 1.0, 0.0).astype(jnp.bfloat16)
        owner = jnp.broadcast_to(request_ref[pl.ds(seq_index, 1), :], (rows, tokens))
        mine = lax.broadcasted_iota(jnp.int32, (rows, tokens), 0) % requests
        live_ref[...] = jnp.where(owner == mine, 1.0, 0.0)

    query = stacked_queries(query_ref, per_group)
    scores = lax.dot_general(
        query, keys_ref[0], (((1,), (1,)), ((), ())), preferred_element_type=jnp.float32
    ) * HD ** (-0.5)
    position = seq_index * local_len + lax.broadcasted_iota(jnp.int32, scores.shape, 1)
    mine = lax.broadcasted_iota(jnp.int32, scores.shape, 0) % requests
    allowed = (mine == request) & (position < len_ref[request])
    scores = jnp.where(allowed, scores, DEAD)
    top = jnp.max(scores, axis=1, keepdims=True)
    weights = jnp.where(allowed, jnp.exp(scores - top), 0.0)
    l_ref[...] += jnp.broadcast_to(jnp.sum(weights, axis=1, keepdims=True), l_ref.shape)
    m_ref[...] = jnp.maximum(m_ref[...], jnp.broadcast_to(top, m_ref.shape))
    o_ref[...] += jnp.dot(
        weights.astype(jnp.bfloat16), values_ref[0], preferred_element_type=jnp.float32
    )


def cache_part(cache_len, query, keys, values, target, request_ids, seq_count):
    requests, local_len, _ = keys.shape
    per_group = query.shape[1] // HD
    rows = requests * per_group
    tokens = target.shape[1]
    f32 = jnp.float32
    fixed = lambda shape: pl.BlockSpec(shape, lambda i: (0,) * len(shape))
    stream = pl.BlockSpec((1, local_len, HD), lambda i: (i, 0, 0))
    return pl.pallas_call(
        functools.partial(cache_kernel, requests, per_group),
        grid=(requests,),
        in_specs=[
            whole(SMEM),
            fixed(query.shape),
            stream,
            stream,
            fixed(target.shape),
            fixed(request_ids.shape),
        ],
        out_specs=[
            fixed((rows, HD)),
            fixed((rows, HD)),
            fixed((rows, HD)),
            fixed((seq_count * TAIL, tokens)),
            fixed((seq_count * TAIL, tokens)),
            fixed((rows, tokens)),
        ],
        out_shape=[
            jax.ShapeDtypeStruct((rows, HD), f32),
            jax.ShapeDtypeStruct((rows, HD), f32),
            jax.ShapeDtypeStruct((rows, HD), f32),
            jax.ShapeDtypeStruct((seq_count * TAIL, tokens), jnp.bfloat16),
            jax.ShapeDtypeStruct((seq_count * TAIL, tokens), jnp.bfloat16),
            jax.ShapeDtypeStruct((rows, tokens), f32),
        ],
        cost_estimate=pl.CostEstimate(
            flops=4 * rows * requests * local_len * HD,
            bytes_accessed=4 * requests * local_len * HD,
            transcendentals=rows * requests * local_len,
        ),
        name="cache_part",
    )(cache_len, query, keys, values, target, request_ids)


def span_kernel(
    per_group,
    parts_ref,
    query_ref,
    o_ref,
    m_ref,
    l_ref,
    place_key_ref,
    place_value_ref,
    live_ref,
    out_ref,
):
    rows = o_ref.shape[0]
    seq_count = out_ref.shape[0]
    total = parts_ref[0].astype(jnp.float32)
    for source in range(1, parts_ref.shape[0]):
        total = total + parts_ref[source].astype(jnp.float32)
    owned = total.astype(jnp.bfloat16)
    span_k, span_v = owned[:, :HD], owned[:, HD:]
    query = stacked_queries(query_ref, per_group)
    live = live_ref[...] > 0.5
    scores = lax.dot_general(
        query, span_k, (((1,), (1,)), ((), ())), preferred_element_type=jnp.float32
    ) * HD ** (-0.5)
    scores = jnp.where(live, scores, DEAD)
    m_cache = m_ref[:, 0:1]
    reference = (
        jnp.maximum(m_cache, jnp.max(scores, axis=1, keepdims=True))
        .astype(jnp.bfloat16)
        .astype(jnp.float32)
    )
    weights = jnp.where(live, jnp.exp(scores - reference), 0.0)
    scale = jnp.exp(m_cache - reference)
    row_sum = scale * l_ref[:, 0:1] + jnp.sum(weights, axis=1, keepdims=True)
    weighted = scale * o_ref[...] + jnp.dot(
        weights.astype(jnp.bfloat16), span_v, preferred_element_type=jnp.float32
    )
    empty = row_sum == 0.0
    shared = jnp.where(empty, 0.0, weighted / jnp.where(empty, 1.0, row_sum)).astype(jnp.bfloat16)
    sum_high = row_sum.astype(jnp.bfloat16).astype(jnp.float32)
    sum_low = row_sum - sum_high
    lane = lax.broadcasted_iota(jnp.int32, (rows, HD), 1)
    row = lax.broadcasted_iota(jnp.int32, (rows, HD), 0)
    spread = jnp.where(lane == row, reference, 0.0)
    spread = jnp.where(lane == row + rows, sum_high, spread)
    spread = jnp.where(lane == row + 2 * rows, sum_low, spread)
    stats = jnp.sum(spread, axis=0, keepdims=True)
    tail = jnp.dot(place_key_ref[...], span_k, preferred_element_type=jnp.float32)
    tail = tail + jnp.dot(place_value_ref[...], span_v, preferred_element_type=jnp.float32)
    within = lax.broadcasted_iota(jnp.int32, tail.shape, 0) % TAIL
    tail = jnp.where(within == 2 * CAP, jnp.broadcast_to(stats, tail.shape), tail)
    out_ref[:, rows:, :] = tail.astype(jnp.bfloat16).reshape(seq_count, TAIL, HD)
    for dest in range(seq_count):
        out_ref[dest, :rows, :] = shared


def span_part(parts, query, cache_state):
    per_group = query.shape[1] // HD
    rows = cache_state[0].shape[0]
    return pl.pallas_call(
        functools.partial(span_kernel, per_group),
        in_specs=[whole()] * (2 + len(cache_state)),
        out_specs=whole(),
        out_shape=jax.ShapeDtypeStruct((parts.shape[0], rows + TAIL, HD), jnp.bfloat16),
        name="span_part",
    )(parts, query, *cache_state)


def out_kernel(requests, message_ref, weight_ref, out_ref):
    seq_count = message_ref.shape[0]
    rows = message_ref.shape[1] - TAIL
    per_group = rows // requests
    tails = message_ref[:, rows:, :].astype(jnp.float32)
    within = lax.broadcasted_iota(jnp.int32, tails.shape, 1)
    stats = jnp.sum(jnp.where(within == 2 * CAP, tails, 0.0), axis=1)
    m = stats[:, :rows]
    sums = stats[:, rows : 2 * rows] + stats[:, 2 * rows : 3 * rows]
    share = jnp.exp(m - jnp.max(m, axis=0, keepdims=True)) * sums
    share = share / jnp.sum(share, axis=0, keepdims=True)
    share = share.T
    total = jnp.zeros((rows, HD), jnp.float32)
    for source in range(seq_count):
        total = total + share[:, source : source + 1] * message_ref[source, :rows, :].astype(
            jnp.float32
        )
    attended = jnp.concatenate(
        [total[h * requests : (h + 1) * requests] for h in range(per_group)], axis=1
    ).astype(jnp.bfloat16)
    projected = jnp.dot(attended, weight_ref[...], preferred_element_type=jnp.float32)
    for dest in range(out_ref.shape[0]):
        out_ref[dest] = projected


def out_part(messages, out_weight, requests, tp_count):
    return pl.pallas_call(
        functools.partial(out_kernel, requests),
        in_specs=[whole()] * 2,
        out_specs=whole(),
        out_shape=jax.ShapeDtypeStruct(
            (tp_count, requests, out_weight.shape[1]), jnp.float32
        ),
        name="out_part",
    )(messages, out_weight)


def per_device(
    decode_query,
    cache_keys,
    cache_values,
    cache_len,
    prefill_rows,
    key_weight,
    value_weight,
    span_request,
    span_target,
    out_weight,
):
    seq_count = lax.axis_size("seq")
    tp_count = lax.axis_size("tp")
    requests = cache_keys.shape[0]
    rows = requests * decode_query.shape[1] // HD
    pre_dev = prefill_rows.shape[0] // seq_count

    partial = project(prefill_rows, key_weight, value_weight)
    partial = partial.reshape(seq_count, pre_dev, 2 * HD)
    parts = lax.all_to_all(partial, "seq", split_axis=0, concat_axis=0, tiled=True)

    targets = span_target.reshape(seq_count, pre_dev)
    request_ids = span_request.reshape(seq_count, pre_dev)
    cache_state = cache_part(
        cache_len, decode_query, cache_keys, cache_values, targets, request_ids, seq_count
    )
    outgoing = span_part(parts, decode_query, cache_state)
    messages = lax.all_to_all(outgoing, "seq", split_axis=0, concat_axis=0, tiled=True)
    appended_keys = messages[:, rows : rows + CAP].reshape(seq_count * CAP, HD)
    appended_values = messages[:, rows + CAP : rows + 2 * CAP].reshape(seq_count * CAP, HD)

    shares = out_part(messages, out_weight, requests, tp_count)
    shares = lax.all_to_all(shares, "tp", split_axis=0, concat_axis=0, tiled=True)
    layer_out = jnp.sum(shares, axis=0).astype(jnp.bfloat16)
    return (layer_out, appended_keys, appended_values)


def solution(mesh):
    placed = (
        P(None, "tp"),
        P(None, "seq", "tp"),
        P(None, "seq", "tp"),
        P(),
        P(None, "seq"),
        P("seq", "tp"),
        P("seq", "tp"),
        P(),
        P(),
        P("tp", "seq"),
    )
    return jax.shard_map(
        per_device,
        mesh=mesh,
        in_specs=placed,
        out_specs=(P(None, "seq"), P("seq", "tp"), P("seq", "tp")),
        check_vma=False,
    )
```

```python
import functools

import jax
import jax.numpy as jnp
from jax import lax
from jax.experimental import pallas as pl
from jax.experimental.pallas import tpu as pltpu
from jax.sharding import PartitionSpec as P

H = 64
KVH = 8
HD = 128
CAP = 2
DEAD = -(2.0**100)
TAIL = 8
VMEM = pltpu.VMEM
SMEM = pltpu.SMEM
MIB = 1 << 20


def whole(space=VMEM):
    return pl.BlockSpec(memory_space=space)


def in_hbm(array):
    return pltpu.with_memory_space_constraint(array, pltpu.HBM)


def project_kernel(rows_hbm, key_hbm, value_hbm, out_ref, rows_ref, weight_ref, sems):
    chunks = sems.shape[0] - 2
    size = rows_ref.shape[0] // chunks
    copies = [
        pltpu.make_async_copy(key_hbm, weight_ref.at[:, :HD], sems.at[0]),
        pltpu.make_async_copy(value_hbm, weight_ref.at[:, HD:], sems.at[1]),
    ] + [
        pltpu.make_async_copy(
            rows_hbm.at[pl.ds(i * size, size)],
            rows_ref.at[pl.ds(i * size, size)],
            sems.at[2 + i],
        )
        for i in range(chunks)
    ]
    for copy in copies:
        copy.start()
    copies[0].wait()
    copies[1].wait()
    weight = weight_ref[...]
    for i in range(chunks):
        copies[2 + i].wait()
        out_ref[pl.ds(i * size, size), :] = jnp.dot(
            rows_ref[pl.ds(i * size, size), :], weight, preferred_element_type=jnp.float32
        ).astype(jnp.bfloat16)


def project(rows, key_weight, value_weight):
    tokens, features = rows.shape
    chunks = 1
    return pl.pallas_call(
        project_kernel,
        in_specs=[whole(pltpu.HBM)] * 3,
        out_specs=whole(),
        out_shape=jax.ShapeDtypeStruct((tokens, 2 * HD), jnp.bfloat16),
        scratch_shapes=[
            VMEM((tokens, features), jnp.bfloat16),
            VMEM((features, 2 * HD), jnp.bfloat16),
            pltpu.SemaphoreType.DMA((2 + chunks,)),
        ],
        compiler_params=pltpu.CompilerParams(vmem_limit_bytes=8 * MIB),
        name="project",
    )(in_hbm(rows), in_hbm(key_weight), in_hbm(value_weight))


def stacked_queries(query_ref, per_group):
    query = query_ref[...]
    return jnp.concatenate(
        [query[:, h * HD : (h + 1) * HD] for h in range(per_group)], axis=0
    )


def cache_kernel(
    requests,
    per_group,
    len_ref,
    query_ref,
    keys_ref,
    values_ref,
    target_ref,
    request_ref,
    o_ref,
    m_ref,
    l_ref,
    place_key_ref,
    place_value_ref,
    live_ref,
):
    request = pl.program_id(0)
    seq_index = lax.axis_index("seq")
    rows = requests * per_group
    local_len = keys_ref.shape[1]

    @pl.when(request == 0)
    def _():
        o_ref[...] = jnp.zeros_like(o_ref)
        l_ref[...] = jnp.zeros_like(l_ref)
        m_ref[...] = jnp.full(m_ref.shape, DEAD, jnp.float32)
        tokens = target_ref.shape[1]
        target = jnp.broadcast_to(target_ref[pl.ds(seq_index, 1), :], (tokens, tokens))
        i = lax.broadcasted_iota(jnp.int32, (tokens, tokens), 0)
        j = lax.broadcasted_iota(jnp.int32, (tokens, tokens), 1)
        column = jnp.sum(jnp.where(i == j, target, 0), axis=1, keepdims=True)
        rank = jnp.sum(
            jnp.where((column == target) & (i < j), 1, 0), axis=0, keepdims=True
        )
        slot = target[0:1, :] * CAP + rank
        count = place_key_ref.shape[0]
        row = lax.broadcasted_iota(jnp.int32, (count, tokens), 0)
        dest, within = row // TAIL, row % TAIL
        wanted = jnp.broadcast_to(slot, (count, tokens))
        is_key = (within < CAP) & (wanted == dest * CAP + within)
        is_value = (within >= CAP) & (within < 2 * CAP) & (wanted == dest * CAP + within - CAP)
        place_key_ref[...] = jnp.where(is_key, 1.0, 0.0).astype(jnp.bfloat16)
        place_value_ref[...] = jnp.where(is_value, 1.0, 0.0).astype(jnp.bfloat16)
        owner = jnp.broadcast_to(request_ref[pl.ds(seq_index, 1), :], (rows, tokens))
        mine = lax.broadcasted_iota(jnp.int32, (rows, tokens), 0) % requests
        live_ref[...] = jnp.where(owner == mine, 1.0, 0.0)

    query = stacked_queries(query_ref, per_group)
    scores = lax.dot_general(
        query, keys_ref[0], (((1,), (1,)), ((), ())), preferred_element_type=jnp.float32
    ) * HD ** (-0.5)
    position = seq_index * local_len + lax.broadcasted_iota(jnp.int32, scores.shape, 1)
    mine = lax.broadcasted_iota(jnp.int32, scores.shape, 0) % requests
    allowed = (mine == request) & (position < len_ref[request])
    scores = jnp.where(allowed, scores, DEAD)
    top = jnp.max(scores, axis=1, keepdims=True)
    weights = jnp.where(allowed, jnp.exp(scores - top), 0.0)
    l_ref[...] += jnp.broadcast_to(jnp.sum(weights, axis=1, keepdims=True), l_ref.shape)
    m_ref[...] = jnp.maximum(m_ref[...], jnp.broadcast_to(top, m_ref.shape))
    o_ref[...] += jnp.dot(
        weights.astype(jnp.bfloat16), values_ref[0], preferred_element_type=jnp.float32
    )


def cache_part(cache_len, query, keys, values, target, request_ids, seq_count):
    requests, local_len, _ = keys.shape
    per_group = query.shape[1] // HD
    rows = requests * per_group
    tokens = target.shape[1]
    f32 = jnp.float32
    fixed = lambda shape: pl.BlockSpec(shape, lambda i: (0,) * len(shape))
    stream = pl.BlockSpec((1, local_len, HD), lambda i: (i, 0, 0))
    return pl.pallas_call(
        functools.partial(cache_kernel, requests, per_group),
        grid=(requests,),
        in_specs=[
            whole(SMEM),
            fixed(query.shape),
            stream,
            stream,
            fixed(target.shape),
            fixed(request_ids.shape),
        ],
        out_specs=[
            fixed((rows, HD)),
            fixed((rows, HD)),
            fixed((rows, HD)),
            fixed((seq_count * TAIL, tokens)),
            fixed((seq_count * TAIL, tokens)),
            fixed((rows, tokens)),
        ],
        out_shape=[
            jax.ShapeDtypeStruct((rows, HD), f32),
            jax.ShapeDtypeStruct((rows, HD), f32),
            jax.ShapeDtypeStruct((rows, HD), f32),
            jax.ShapeDtypeStruct((seq_count * TAIL, tokens), jnp.bfloat16),
            jax.ShapeDtypeStruct((seq_count * TAIL, tokens), jnp.bfloat16),
            jax.ShapeDtypeStruct((rows, tokens), f32),
        ],
        cost_estimate=pl.CostEstimate(
            flops=4 * rows * requests * local_len * HD,
            bytes_accessed=4 * requests * local_len * HD,
            transcendentals=rows * requests * local_len,
        ),
        compiler_params=pltpu.CompilerParams(vmem_limit_bytes=16 * MIB),
        name="cache_part",
    )(cache_len, query, in_hbm(keys), in_hbm(values), target, request_ids)


def span_kernel(
    per_group,
    parts_ref,
    query_ref,
    o_ref,
    m_ref,
    l_ref,
    place_key_ref,
    place_value_ref,
    live_ref,
    out_ref,
):
    rows = o_ref.shape[0]
    seq_count = out_ref.shape[0]
    total = parts_ref[0].astype(jnp.float32)
    for source in range(1, parts_ref.shape[0]):
        total = total + parts_ref[source].astype(jnp.float32)
    owned = total.astype(jnp.bfloat16)
    span_k, span_v = owned[:, :HD], owned[:, HD:]
    query = stacked_queries(query_ref, per_group)
    live = live_ref[...] > 0.5
    scores = lax.dot_general(
        query, span_k, (((1,), (1,)), ((), ())), preferred_element_type=jnp.float32
    ) * HD ** (-0.5)
    scores = jnp.where(live, scores, DEAD)
    m_cache = m_ref[:, 0:1]
    reference = (
        jnp.maximum(m_cache, jnp.max(scores, axis=1, keepdims=True))
        .astype(jnp.bfloat16)
        .astype(jnp.float32)
    )
    weights = jnp.where(live, jnp.exp(scores - reference), 0.0)
    scale = jnp.exp(m_cache - reference)
    row_sum = scale * l_ref[:, 0:1] + jnp.sum(weights, axis=1, keepdims=True)
    weighted = scale * o_ref[...] + jnp.dot(
        weights.astype(jnp.bfloat16), span_v, preferred_element_type=jnp.float32
    )
    empty = row_sum == 0.0
    shared = jnp.where(empty, 0.0, weighted / jnp.where(empty, 1.0, row_sum)).astype(jnp.bfloat16)
    sum_high = row_sum.astype(jnp.bfloat16).astype(jnp.float32)
    sum_low = row_sum - sum_high
    lane = lax.broadcasted_iota(jnp.int32, (rows, HD), 1)
    row = lax.broadcasted_iota(jnp.int32, (rows, HD), 0)
    spread = jnp.where(lane == row, reference, 0.0)
    spread = jnp.where(lane == row + rows, sum_high, spread)
    spread = jnp.where(lane == row + 2 * rows, sum_low, spread)
    stats = jnp.sum(spread, axis=0, keepdims=True)
    tail = jnp.dot(place_key_ref[...], span_k, preferred_element_type=jnp.float32)
    tail = tail + jnp.dot(place_value_ref[...], span_v, preferred_element_type=jnp.float32)
    within = lax.broadcasted_iota(jnp.int32, tail.shape, 0) % TAIL
    tail = jnp.where(within == 2 * CAP, jnp.broadcast_to(stats, tail.shape), tail)
    out_ref[:, rows:, :] = tail.astype(jnp.bfloat16).reshape(seq_count, TAIL, HD)
    for dest in range(seq_count):
        out_ref[dest, :rows, :] = shared


def span_part(parts, query, cache_state):
    per_group = query.shape[1] // HD
    rows = cache_state[0].shape[0]
    return pl.pallas_call(
        functools.partial(span_kernel, per_group),
        in_specs=[whole()] * (2 + len(cache_state)),
        out_specs=whole(),
        out_shape=jax.ShapeDtypeStruct((parts.shape[0], rows + TAIL, HD), jnp.bfloat16),
        compiler_params=pltpu.CompilerParams(vmem_limit_bytes=8 * MIB),
        name="span_part",
    )(parts, query, *cache_state)


def out_kernel(
    requests, message_ref, weight_ref, out_ref, key_hbm, value_hbm, key_ref, value_ref, sems
):
    seq_count = message_ref.shape[0]
    rows = message_ref.shape[1] - TAIL
    per_group = rows // requests
    tails = message_ref[:, rows:, :]
    key_ref[...] = tails[:, :CAP].reshape(key_ref.shape)
    value_ref[...] = tails[:, CAP : 2 * CAP].reshape(value_ref.shape)
    copies = [
        pltpu.make_async_copy(key_ref, key_hbm, sems.at[0]),
        pltpu.make_async_copy(value_ref, value_hbm, sems.at[1]),
    ]
    for copy in copies:
        copy.start()
    tails = tails.astype(jnp.float32)
    within = lax.broadcasted_iota(jnp.int32, tails.shape, 1)
    stats = jnp.sum(jnp.where(within == 2 * CAP, tails, 0.0), axis=1)
    m = stats[:, :rows]
    sums = stats[:, rows : 2 * rows] + stats[:, 2 * rows : 3 * rows]
    share = jnp.exp(m - jnp.max(m, axis=0, keepdims=True)) * sums
    share = share / jnp.sum(share, axis=0, keepdims=True)
    share = share.T
    total = jnp.zeros((rows, HD), jnp.float32)
    for source in range(seq_count):
        total = total + share[:, source : source + 1] * message_ref[source, :rows, :].astype(
            jnp.float32
        )
    attended = jnp.concatenate(
        [total[h * requests : (h + 1) * requests] for h in range(per_group)], axis=1
    ).astype(jnp.bfloat16)
    projected = jnp.dot(attended, weight_ref[...], preferred_element_type=jnp.float32)
    for dest in range(out_ref.shape[0]):
        out_ref[dest] = projected
    for copy in copies:
        copy.wait()


def out_part(messages, out_weight, requests, tp_count):
    slots = jax.ShapeDtypeStruct((messages.shape[0] * CAP, HD), jnp.bfloat16)
    return pl.pallas_call(
        functools.partial(out_kernel, requests),
        in_specs=[whole()] * 2,
        out_specs=[whole(), whole(pltpu.HBM), whole(pltpu.HBM)],
        out_shape=[
            jax.ShapeDtypeStruct((tp_count, requests, out_weight.shape[1]), jnp.float32),
            slots,
            slots,
        ],
        scratch_shapes=[
            VMEM(slots.shape, slots.dtype),
            VMEM(slots.shape, slots.dtype),
            pltpu.SemaphoreType.DMA((2,)),
        ],
        compiler_params=pltpu.CompilerParams(vmem_limit_bytes=8 * MIB),
        name="out_part",
    )(messages, out_weight)


def per_device(
    decode_query,
    cache_keys,
    cache_values,
    cache_len,
    prefill_rows,
    key_weight,
    value_weight,
    span_request,
    span_target,
    out_weight,
):
    seq_count = lax.axis_size("seq")
    tp_count = lax.axis_size("tp")
    requests = cache_keys.shape[0]
    rows = requests * decode_query.shape[1] // HD
    pre_dev = prefill_rows.shape[0] // seq_count

    partial = project(prefill_rows, key_weight, value_weight)
    partial = partial.reshape(seq_count, pre_dev, 2 * HD)
    parts = lax.all_to_all(partial, "seq", split_axis=0, concat_axis=0, tiled=True)

    targets = span_target.reshape(seq_count, pre_dev)
    request_ids = span_request.reshape(seq_count, pre_dev)
    cache_state = cache_part(
        cache_len, decode_query, cache_keys, cache_values, targets, request_ids, seq_count
    )
    outgoing = span_part(parts, decode_query, cache_state)
    messages = lax.all_to_all(outgoing, "seq", split_axis=0, concat_axis=0, tiled=True)
    shares, appended_keys, appended_values = out_part(
        messages, out_weight, requests, tp_count
    )
    shares = lax.all_to_all(shares, "tp", split_axis=0, concat_axis=0, tiled=True)
    layer_out = jnp.sum(shares, axis=0).astype(jnp.bfloat16)
    return (layer_out, appended_keys, appended_values)


def solution(mesh):
    placed = (
        P(None, "tp"),
        P(None, "seq", "tp"),
        P(None, "seq", "tp"),
        P(),
        P(None, "seq"),
        P("seq", "tp"),
        P("seq", "tp"),
        P(),
        P(),
        P("tp", "seq"),
    )
    return jax.shard_map(
        per_device,
        mesh=mesh,
        in_specs=placed,
        out_specs=(P(None, "seq"), P("seq", "tp"), P("seq", "tp")),
        check_vma=False,
    )
```

```python
import functools

import jax
import jax.numpy as jnp
from jax import lax
from jax.experimental import pallas as pl
from jax.experimental.pallas import tpu as pltpu
from jax.sharding import PartitionSpec as P

H = 64
KVH = 8
HD = 128
CAP = 2
DEAD = -(2.0**100)
NY = 4
NZ = 8
TAIL = 8
VMEM = pltpu.VMEM
SMEM = pltpu.SMEM
MIB = 1 << 20


def whole(space=VMEM):
    return pl.BlockSpec(memory_space=space)


def in_hbm(array):
    return pltpu.with_memory_space_constraint(array, pltpu.HBM)


def project_kernel(
    rows_hbm, key_hbm, value_hbm, own_ref, to1_ref, to2_ref, to3_ref, rows_ref, weight_ref, sems
):
    copies = [
        pltpu.make_async_copy(key_hbm, weight_ref.at[:, :HD], sems.at[0]),
        pltpu.make_async_copy(value_hbm, weight_ref.at[:, HD:], sems.at[1]),
        pltpu.make_async_copy(rows_hbm, rows_ref, sems.at[2]),
    ]
    for copy in copies:
        copy.start()
    for copy in copies:
        copy.wait()
    weight = weight_ref[...]
    y = lax.axis_index("seq") // NZ
    size = own_ref.shape[0]
    for k, ref in enumerate((own_ref, to1_ref, to2_ref, to3_ref)):
        first = pl.multiple_of(lax.rem(y + k, NY) * size, size)
        ref[...] = jnp.dot(
            rows_ref[pl.ds(first, size), :], weight, preferred_element_type=jnp.float32
        ).astype(jnp.bfloat16)


def project(rows, key_weight, value_weight):
    tokens, features = rows.shape
    return pl.pallas_call(
        project_kernel,
        in_specs=[whole(pltpu.HBM)] * 3,
        out_specs=[whole()] * NY,
        out_shape=[jax.ShapeDtypeStruct((tokens // NY, 2 * HD), jnp.bfloat16)] * NY,
        scratch_shapes=[
            VMEM((tokens, features), jnp.bfloat16),
            VMEM((features, 2 * HD), jnp.bfloat16),
            pltpu.SemaphoreType.DMA((3,)),
        ],
        compiler_params=pltpu.CompilerParams(vmem_limit_bytes=8 * MIB),
        name="project",
    )(in_hbm(rows), in_hbm(key_weight), in_hbm(value_weight))


def fold_kernel(after_ref, own_ref, from1_ref, from2_ref, from3_ref, out_ref):
    total = own_ref[...].astype(jnp.float32)
    for ref in (from1_ref, from2_ref, from3_ref):
        total = total + ref[...].astype(jnp.float32)
    out_ref[...] = total.astype(jnp.bfloat16)


def fold(after, parts):
    return pl.pallas_call(
        fold_kernel,
        in_specs=[whole()] * 5,
        out_specs=whole(),
        out_shape=jax.ShapeDtypeStruct(parts[0].shape, jnp.bfloat16),
        compiler_params=pltpu.CompilerParams(vmem_limit_bytes=8 * MIB),
        name="fold",
    )(after, *parts)


def stacked_queries(query_ref, per_group):
    query = query_ref[...]
    return jnp.concatenate(
        [query[:, h * HD : (h + 1) * HD] for h in range(per_group)], axis=0
    )


def cache_kernel(
    requests,
    per_group,
    len_hbm,
    query_hbm,
    target_hbm,
    request_hbm,
    keys_hbm,
    values_hbm,
    o_ref,
    m_ref,
    l_ref,
    place_key_ref,
    place_value_ref,
    live_ref,
    stacked_ref,
    len_ref,
    query_ref,
    target_ref,
    request_ref,
    keys_ref,
    values_ref,
    query_rows,
    o_rows,
    m_rows,
    l_rows,
    small_sems,
    sems,
):
    seq_index = lax.axis_index("seq")
    rows = requests * per_group
    local_len = keys_ref.shape[1]
    tokens = live_ref.shape[1]
    small = [
        pltpu.make_async_copy(source, dest, small_sems.at[i])
        for i, (source, dest) in enumerate(
            (
                (len_hbm, len_ref),
                (query_hbm, query_ref),
                (target_hbm, target_ref),
                (request_hbm, request_ref),
            )
        )
    ]
    key_copies = [
        pltpu.make_async_copy(keys_hbm.at[r], keys_ref.at[r], sems.at[0, r])
        for r in range(requests)
    ]
    value_copies = [
        pltpu.make_async_copy(values_hbm.at[r], values_ref.at[r], sems.at[1, r])
        for r in range(requests)
    ]
    for copy in small:
        copy.start()
    for r in range(requests):
        key_copies[r].start()
        value_copies[r].start()
    for copy in small:
        copy.wait()

    per_tile = HD // tokens
    first = pl.multiple_of(seq_index // per_tile * HD, HD)
    shift = lax.rem(HD - lax.rem(seq_index, per_tile) * tokens, HD)

    def own(ref):
        tile = jnp.broadcast_to(ref[:, pl.ds(first, HD)], (8, HD))
        return pltpu.roll(tile, shift, 1)[0:1, :tokens]

    target_row = own(target_ref)
    target = jnp.broadcast_to(target_row, (tokens, tokens))
    i = lax.broadcasted_iota(jnp.int32, (tokens, tokens), 0)
    j = lax.broadcasted_iota(jnp.int32, (tokens, tokens), 1)
    column = jnp.sum(jnp.where(i == j, target, 0), axis=1, keepdims=True)
    rank = jnp.sum(jnp.where((column == target) & (i < j), 1, 0), axis=0, keepdims=True)
    slot = target_row * CAP + rank
    count = place_key_ref.shape[0]
    row = lax.broadcasted_iota(jnp.int32, (count, tokens), 0)
    dest, within = row // TAIL, row % TAIL
    wanted = jnp.broadcast_to(slot, (count, tokens))
    is_key = (within < CAP) & (wanted == dest * CAP + within)
    is_value = (within >= CAP) & (within < 2 * CAP) & (wanted == dest * CAP + within - CAP)
    place_key_ref[...] = jnp.where(is_key, 1.0, 0.0).astype(jnp.bfloat16)
    place_value_ref[...] = jnp.where(is_value, 1.0, 0.0).astype(jnp.bfloat16)
    owner = jnp.broadcast_to(own(request_ref), (rows, tokens))
    mine = lax.broadcasted_iota(jnp.int32, (rows, tokens), 0) % requests
    live_ref[...] = jnp.where(owner == mine, 1.0, 0.0)

    stacked = stacked_queries(query_ref, per_group)
    stacked_ref[...] = stacked
    query_rows[...] = stacked.astype(jnp.float32)
    for r in range(requests):
        query = query_rows[pl.ds(r, per_group, stride=requests), :].astype(jnp.bfloat16)
        key_copies[r].wait()
        scores = lax.dot_general(
            query, keys_ref[r], (((1,), (1,)), ((), ())), preferred_element_type=jnp.float32
        ) * HD ** (-0.5)
        position = seq_index * local_len + lax.broadcasted_iota(jnp.int32, scores.shape, 1)
        allowed = position < len_ref[r]
        scores = jnp.where(allowed, scores, DEAD)
        top = jnp.max(scores, axis=1, keepdims=True)
        weights = jnp.where(allowed, jnp.exp(scores - top), 0.0)
        own_rows = pl.ds(r * per_group, per_group)
        l_rows[own_rows, :] = jnp.broadcast_to(
            jnp.sum(weights, axis=1, keepdims=True), (per_group, HD)
        )
        m_rows[own_rows, :] = jnp.broadcast_to(top, (per_group, HD))
        value_copies[r].wait()
        o_rows[own_rows, :] = jnp.dot(
            weights.astype(jnp.bfloat16), values_ref[r], preferred_element_type=jnp.float32
        )
    for h in range(per_group):
        to = pl.ds(h * requests, requests)
        of = pl.ds(h, requests, stride=per_group)
        o_ref[to, :] = o_rows[of, :]
        m_ref[to, :] = m_rows[of, :]
        l_ref[to, :] = l_rows[of, :]


def cache_part(cache_len, query, keys, values, target, request_ids, seq_count):
    requests, local_len, _ = keys.shape
    per_group = query.shape[1] // HD
    rows = requests * per_group
    tokens = target.shape[1] // seq_count
    f32 = jnp.float32
    table = jax.ShapeDtypeStruct((rows, HD), f32)
    place = jax.ShapeDtypeStruct((seq_count * TAIL, tokens), jnp.bfloat16)
    operands = (cache_len, query, target, request_ids, keys, values)
    return pl.pallas_call(
        functools.partial(cache_kernel, requests, per_group),
        in_specs=[whole(pltpu.HBM)] * 6,
        out_specs=[whole()] * 7,
        out_shape=[
            table,
            table,
            table,
            place,
            place,
            jax.ShapeDtypeStruct((rows, tokens), f32),
            jax.ShapeDtypeStruct((rows, HD), query.dtype),
        ],
        scratch_shapes=[SMEM(cache_len.shape, cache_len.dtype)]
        + [VMEM(a.shape, a.dtype) for a in operands[1:]]
        + [VMEM((rows, HD), f32)] * 4
        + [pltpu.SemaphoreType.DMA((4,)), pltpu.SemaphoreType.DMA((2, requests))],
        cost_estimate=pl.CostEstimate(
            flops=4 * rows * local_len * HD,
            bytes_accessed=4 * requests * local_len * HD,
            transcendentals=rows * local_len,
        ),
        compiler_params=pltpu.CompilerParams(vmem_limit_bytes=16 * MIB),
        name="cache_part",
    )(*[in_hbm(a) for a in operands])


def span_kernel(
    parts_ref,
    o_ref,
    m_ref,
    l_ref,
    place_key_ref,
    place_value_ref,
    live_ref,
    query_ref,
    out_ref,
):
    rows = o_ref.shape[0]
    seq_count = out_ref.shape[0]
    total = parts_ref[0].astype(jnp.float32)
    for source in range(1, parts_ref.shape[0]):
        total = total + parts_ref[source].astype(jnp.float32)
    owned = total.astype(jnp.bfloat16)
    span_k, span_v = owned[:, :HD], owned[:, HD:]
    live = live_ref[...] > 0.5
    scores = lax.dot_general(
        query_ref[...], span_k, (((1,), (1,)), ((), ())), preferred_element_type=jnp.float32
    ) * HD ** (-0.5)
    scores = jnp.where(live, scores, DEAD)
    m_cache = m_ref[:, 0:1]
    reference = (
        jnp.maximum(m_cache, jnp.max(scores, axis=1, keepdims=True))
        .astype(jnp.bfloat16)
        .astype(jnp.float32)
    )
    weights = jnp.where(live, jnp.exp(scores - reference), 0.0)
    scale = jnp.exp(m_cache - reference)
    row_sum = scale * l_ref[:, 0:1] + jnp.sum(weights, axis=1, keepdims=True)
    weighted = scale * o_ref[...] + jnp.dot(
        weights.astype(jnp.bfloat16), span_v, preferred_element_type=jnp.float32
    )
    empty = row_sum == 0.0
    shared = jnp.where(empty, 0.0, weighted / jnp.where(empty, 1.0, row_sum)).astype(jnp.bfloat16)
    sum_high = row_sum.astype(jnp.bfloat16).astype(jnp.float32)
    sum_low = row_sum - sum_high
    lane = lax.broadcasted_iota(jnp.int32, (rows, HD), 1)
    row = lax.broadcasted_iota(jnp.int32, (rows, HD), 0)
    spread = jnp.where(lane == row, reference, 0.0)
    spread = jnp.where(lane == row + rows, sum_high, spread)
    spread = jnp.where(lane == row + 2 * rows, sum_low, spread)
    stats = jnp.sum(spread, axis=0, keepdims=True)
    tail = jnp.dot(place_key_ref[...], span_k, preferred_element_type=jnp.float32)
    tail = tail + jnp.dot(place_value_ref[...], span_v, preferred_element_type=jnp.float32)
    within = lax.broadcasted_iota(jnp.int32, tail.shape, 0) % TAIL
    tail = jnp.where(within == 2 * CAP, jnp.broadcast_to(stats, tail.shape), tail)
    out_ref[:, rows:, :] = tail.astype(jnp.bfloat16).reshape(seq_count, TAIL, HD)
    for dest in range(seq_count):
        out_ref[dest, :rows, :] = shared


def span_part(parts, cache_state, seq_count):
    rows = cache_state[0].shape[0]
    return pl.pallas_call(
        span_kernel,
        in_specs=[whole()] * (1 + len(cache_state)),
        out_specs=whole(),
        out_shape=jax.ShapeDtypeStruct((seq_count, rows + TAIL, HD), jnp.bfloat16),
        compiler_params=pltpu.CompilerParams(vmem_limit_bytes=8 * MIB),
        name="span_part",
    )(parts, *cache_state)


def out_kernel(
    requests, message_ref, weight_ref, out_ref, key_hbm, value_hbm, key_ref, value_ref, sems
):
    seq_count = message_ref.shape[0]
    rows = message_ref.shape[1] - TAIL
    per_group = rows // requests
    tails = message_ref[:, rows:, :]
    key_ref[...] = tails[:, :CAP].reshape(key_ref.shape)
    value_ref[...] = tails[:, CAP : 2 * CAP].reshape(value_ref.shape)
    copies = [
        pltpu.make_async_copy(key_ref, key_hbm, sems.at[0]),
        pltpu.make_async_copy(value_ref, value_hbm, sems.at[1]),
    ]
    for copy in copies:
        copy.start()
    tails = tails.astype(jnp.float32)
    within = lax.broadcasted_iota(jnp.int32, tails.shape, 1)
    stats = jnp.sum(jnp.where(within == 2 * CAP, tails, 0.0), axis=1)
    m = stats[:, :rows]
    sums = stats[:, rows : 2 * rows] + stats[:, 2 * rows : 3 * rows]
    share = jnp.exp(m - jnp.max(m, axis=0, keepdims=True)) * sums
    share = share / jnp.sum(share, axis=0, keepdims=True)
    share = share.T
    total = jnp.zeros((rows, HD), jnp.float32)
    for source in range(seq_count):
        total = total + share[:, source : source + 1] * message_ref[source, :rows, :].astype(
            jnp.float32
        )
    attended = jnp.concatenate(
        [total[h * requests : (h + 1) * requests] for h in range(per_group)], axis=1
    ).astype(jnp.bfloat16)
    projected = jnp.dot(attended, weight_ref[...], preferred_element_type=jnp.float32)
    for dest in range(out_ref.shape[0]):
        out_ref[dest] = projected
    for copy in copies:
        copy.wait()


def out_part(messages, out_weight, requests, tp_count):
    slots = jax.ShapeDtypeStruct((messages.shape[0] * CAP, HD), jnp.bfloat16)
    return pl.pallas_call(
        functools.partial(out_kernel, requests),
        in_specs=[whole()] * 2,
        out_specs=[whole(), whole(pltpu.HBM), whole(pltpu.HBM)],
        out_shape=[
            jax.ShapeDtypeStruct((tp_count, requests, out_weight.shape[1]), jnp.float32),
            slots,
            slots,
        ],
        scratch_shapes=[
            VMEM(slots.shape, slots.dtype),
            VMEM(slots.shape, slots.dtype),
            pltpu.SemaphoreType.DMA((2,)),
        ],
        compiler_params=pltpu.CompilerParams(vmem_limit_bytes=8 * MIB),
        name="out_part",
    )(messages, out_weight)


def per_device(
    decode_query,
    cache_keys,
    cache_values,
    cache_len,
    prefill_rows,
    key_weight,
    value_weight,
    span_request,
    span_target,
    out_weight,
):
    seq_count = lax.axis_size("seq")
    tp_count = lax.axis_size("tp")
    requests = cache_keys.shape[0]
    rows = requests * decode_query.shape[1] // HD
    pre_dev = prefill_rows.shape[0] // seq_count

    own, *sent = project(prefill_rows, key_weight, value_weight)
    seq = [(y, z) for y in range(NY) for z in range(NZ)]
    came = [
        lax.ppermute(part, "seq", [(y * NZ + z, (y + k + 1) % NY * NZ + z) for y, z in seq])
        for k, part in enumerate(sent)
    ]
    targets = span_target.T
    request_ids = span_request.reshape(targets.shape)
    cache_state = cache_part(
        cache_len, decode_query, cache_keys, cache_values, targets, request_ids, seq_count
    )
    partial = fold(cache_state[0], [own, *came]).reshape(NZ, pre_dev, 2 * HD)
    parts = lax.all_to_all(
        partial,
        "seq",
        split_axis=0,
        concat_axis=0,
        tiled=True,
        axis_index_groups=[[y * NZ + z for z in range(NZ)] for y in range(NY)],
    )
    outgoing = span_part(parts, cache_state, seq_count)
    messages = lax.all_to_all(outgoing, "seq", split_axis=0, concat_axis=0, tiled=True)
    shares, appended_keys, appended_values = out_part(
        messages, out_weight, requests, tp_count
    )
    shares = lax.all_to_all(shares, "tp", split_axis=0, concat_axis=0, tiled=True)
    layer_out = jnp.sum(shares, axis=0).astype(jnp.bfloat16)
    return (layer_out, appended_keys, appended_values)


def solution(mesh):
    placed = (
        P(None, "tp"),
        P(None, "seq", "tp"),
        P(None, "seq", "tp"),
        P(),
        P(None, "seq"),
        P("seq", "tp"),
        P("seq", "tp"),
        P(),
        P(),
        P("tp", "seq"),
    )
    return jax.shard_map(
        per_device,
        mesh=mesh,
        in_specs=placed,
        out_specs=(P(None, "seq"), P("seq", "tp"), P("seq", "tp")),
        check_vma=False,
    )
```

```python
import functools

import jax
import jax.numpy as jnp
from jax import lax
from jax.experimental import pallas as pl
from jax.experimental.pallas import tpu as pltpu
from jax.sharding import PartitionSpec as P

H = 64
KVH = 8
HD = 128
CAP = 2
DEAD = -(2.0**100)
NY = 4
NZ = 8
Y_STEPS = (1, 3, 2)
TAIL = 8
VMEM = pltpu.VMEM
SMEM = pltpu.SMEM
MIB = 1 << 20


def whole(space=VMEM):
    return pl.BlockSpec(memory_space=space)


def in_hbm(array):
    return pltpu.with_memory_space_constraint(array, pltpu.HBM)


def project_kernel(
    rows_hbm, key_hbm, value_hbm, own_ref, to1_ref, to2_ref, to3_ref, rows_ref, weight_ref, sems
):
    copies = [
        pltpu.make_async_copy(key_hbm, weight_ref.at[:, :HD], sems.at[0]),
        pltpu.make_async_copy(value_hbm, weight_ref.at[:, HD:], sems.at[1]),
        pltpu.make_async_copy(rows_hbm, rows_ref, sems.at[2]),
    ]
    for copy in copies:
        copy.start()
    for copy in copies:
        copy.wait()
    weight = weight_ref[...]
    y = lax.axis_index("seq") // NZ
    size = own_ref.shape[0]
    for k, ref in zip((0,) + Y_STEPS, (own_ref, to1_ref, to2_ref, to3_ref)):
        first = pl.multiple_of(lax.rem(y + k, NY) * size, size)
        ref[...] = jnp.dot(
            rows_ref[pl.ds(first, size), :], weight, preferred_element_type=jnp.float32
        ).astype(jnp.bfloat16)


def project(rows, key_weight, value_weight):
    tokens, features = rows.shape
    return pl.pallas_call(
        project_kernel,
        in_specs=[whole(pltpu.HBM)] * 3,
        out_specs=[whole()] * NY,
        out_shape=[jax.ShapeDtypeStruct((tokens // NY, 2 * HD), jnp.bfloat16)] * NY,
        scratch_shapes=[
            VMEM((tokens, features), jnp.bfloat16),
            VMEM((features, 2 * HD), jnp.bfloat16),
            pltpu.SemaphoreType.DMA((3,)),
        ],
        compiler_params=pltpu.CompilerParams(vmem_limit_bytes=8 * MIB),
        name="project",
    )(in_hbm(rows), in_hbm(key_weight), in_hbm(value_weight))


def fold_kernel(after_ref, own_ref, from1_ref, from2_ref, from3_ref, out_ref):
    total = own_ref[...].astype(jnp.float32)
    for ref in (from1_ref, from2_ref, from3_ref):
        total = total + ref[...].astype(jnp.float32)
    out_ref[...] = total.astype(jnp.bfloat16)


def fold(after, parts):
    return pl.pallas_call(
        fold_kernel,
        in_specs=[whole()] * 5,
        out_specs=whole(),
        out_shape=jax.ShapeDtypeStruct(parts[0].shape, jnp.bfloat16),
        compiler_params=pltpu.CompilerParams(vmem_limit_bytes=8 * MIB),
        name="fold",
    )(after, *parts)


def stacked_queries(query_ref, per_group):
    query = query_ref[...]
    return jnp.concatenate(
        [query[:, h * HD : (h + 1) * HD] for h in range(per_group)], axis=0
    )


def cache_kernel(
    requests,
    per_group,
    len_hbm,
    query_hbm,
    target_hbm,
    request_hbm,
    keys_hbm,
    values_hbm,
    o_ref,
    m_ref,
    l_ref,
    place_key_ref,
    place_value_ref,
    live_ref,
    stacked_ref,
    len_ref,
    query_ref,
    target_ref,
    request_ref,
    keys_ref,
    values_ref,
    query_rows,
    o_rows,
    m_rows,
    l_rows,
    small_sems,
    sems,
):
    seq_index = lax.axis_index("seq")
    rows = requests * per_group
    local_len = keys_ref.shape[1]
    tokens = live_ref.shape[1]
    small = [
        pltpu.make_async_copy(source, dest, small_sems.at[i])
        for i, (source, dest) in enumerate(
            (
                (len_hbm, len_ref),
                (query_hbm, query_ref),
                (target_hbm, target_ref),
                (request_hbm, request_ref),
            )
        )
    ]
    key_copies = [
        pltpu.make_async_copy(keys_hbm.at[r], keys_ref.at[r], sems.at[0, r])
        for r in range(requests)
    ]
    value_copies = [
        pltpu.make_async_copy(values_hbm.at[r], values_ref.at[r], sems.at[1, r])
        for r in range(requests)
    ]
    for copy in small:
        copy.start()
    for r in range(requests):
        key_copies[r].start()
        value_copies[r].start()
    for copy in small:
        copy.wait()

    per_tile = HD // tokens
    first = pl.multiple_of(seq_index // per_tile * HD, HD)
    shift = lax.rem(HD - lax.rem(seq_index, per_tile) * tokens, HD)

    def own(ref):
        tile = jnp.broadcast_to(ref[:, pl.ds(first, HD)], (8, HD))
        return pltpu.roll(tile, shift, 1)[0:1, :tokens]

    target_row = own(target_ref)
    target = jnp.broadcast_to(target_row, (tokens, tokens))
    i = lax.broadcasted_iota(jnp.int32, (tokens, tokens), 0)
    j = lax.broadcasted_iota(jnp.int32, (tokens, tokens), 1)
    column = jnp.sum(jnp.where(i == j, target, 0), axis=1, keepdims=True)
    rank = jnp.sum(jnp.where((column == target) & (i < j), 1, 0), axis=0, keepdims=True)
    slot = target_row * CAP + rank
    count = place_key_ref.shape[0]
    row = lax.broadcasted_iota(jnp.int32, (count, tokens), 0)
    dest, within = row // TAIL, row % TAIL
    wanted = jnp.broadcast_to(slot, (count, tokens))
    is_key = (within < CAP) & (wanted == dest * CAP + within)
    is_value = (within >= CAP) & (within < 2 * CAP) & (wanted == dest * CAP + within - CAP)
    place_key_ref[...] = jnp.where(is_key, 1.0, 0.0).astype(jnp.bfloat16)
    place_value_ref[...] = jnp.where(is_value, 1.0, 0.0).astype(jnp.bfloat16)
    owner = jnp.broadcast_to(own(request_ref), (rows, tokens))
    mine = lax.broadcasted_iota(jnp.int32, (rows, tokens), 0) % requests
    live_ref[...] = jnp.where(owner == mine, 1.0, 0.0)

    stacked = stacked_queries(query_ref, per_group)
    stacked_ref[...] = stacked
    query_rows[...] = stacked.astype(jnp.float32)
    for r in range(requests):
        query = query_rows[pl.ds(r, per_group, stride=requests), :].astype(jnp.bfloat16)
        key_copies[r].wait()
        scores = lax.dot_general(
            query, keys_ref[r], (((1,), (1,)), ((), ())), preferred_element_type=jnp.float32
        ) * HD ** (-0.5)
        position = seq_index * local_len + lax.broadcasted_iota(jnp.int32, scores.shape, 1)
        allowed = position < len_ref[r]
        scores = jnp.where(allowed, scores, DEAD)
        top = jnp.max(scores, axis=1, keepdims=True)
        weights = jnp.where(allowed, jnp.exp(scores - top), 0.0)
        own_rows = pl.ds(r * per_group, per_group)
        l_rows[own_rows, :] = jnp.broadcast_to(
            jnp.sum(weights, axis=1, keepdims=True), (per_group, HD)
        )
        m_rows[own_rows, :] = jnp.broadcast_to(top, (per_group, HD))
        value_copies[r].wait()
        o_rows[own_rows, :] = jnp.dot(
            weights.astype(jnp.bfloat16), values_ref[r], preferred_element_type=jnp.float32
        )
    for h in range(per_group):
        to = pl.ds(h * requests, requests)
        of = pl.ds(h, requests, stride=per_group)
        o_ref[to, :] = o_rows[of, :]
        m_ref[to, :] = m_rows[of, :]
        l_ref[to, :] = l_rows[of, :]


def cache_part(cache_len, query, keys, values, target, request_ids, seq_count):
    requests, local_len, _ = keys.shape
    per_group = query.shape[1] // HD
    rows = requests * per_group
    tokens = target.shape[1] // seq_count
    f32 = jnp.float32
    table = jax.ShapeDtypeStruct((rows, HD), f32)
    place = jax.ShapeDtypeStruct((seq_count * TAIL, tokens), jnp.bfloat16)
    operands = (cache_len, query, target, request_ids, keys, values)
    return pl.pallas_call(
        functools.partial(cache_kernel, requests, per_group),
        in_specs=[whole(pltpu.HBM)] * 6,
        out_specs=[whole()] * 7,
        out_shape=[
            table,
            table,
            table,
            place,
            place,
            jax.ShapeDtypeStruct((rows, tokens), f32),
            jax.ShapeDtypeStruct((rows, HD), query.dtype),
        ],
        scratch_shapes=[SMEM(cache_len.shape, cache_len.dtype)]
        + [VMEM(a.shape, a.dtype) for a in operands[1:]]
        + [VMEM((rows, HD), f32)] * 4
        + [pltpu.SemaphoreType.DMA((4,)), pltpu.SemaphoreType.DMA((2, requests))],
        cost_estimate=pl.CostEstimate(
            flops=4 * rows * local_len * HD,
            bytes_accessed=4 * requests * local_len * HD,
            transcendentals=rows * local_len,
        ),
        compiler_params=pltpu.CompilerParams(vmem_limit_bytes=16 * MIB),
        name="cache_part",
    )(*[in_hbm(a) for a in operands])


def span_kernel(
    parts_ref,
    o_ref,
    m_ref,
    l_ref,
    place_key_ref,
    place_value_ref,
    live_ref,
    query_ref,
    out_ref,
):
    rows = o_ref.shape[0]
    seq_count = out_ref.shape[0]
    total = parts_ref[0].astype(jnp.float32)
    for source in range(1, parts_ref.shape[0]):
        total = total + parts_ref[source].astype(jnp.float32)
    owned = total.astype(jnp.bfloat16)
    span_k, span_v = owned[:, :HD], owned[:, HD:]
    live = live_ref[...] > 0.5
    scores = lax.dot_general(
        query_ref[...], span_k, (((1,), (1,)), ((), ())), preferred_element_type=jnp.float32
    ) * HD ** (-0.5)
    scores = jnp.where(live, scores, DEAD)
    m_cache = m_ref[:, 0:1]
    reference = (
        jnp.maximum(m_cache, jnp.max(scores, axis=1, keepdims=True))
        .astype(jnp.bfloat16)
        .astype(jnp.float32)
    )
    weights = jnp.where(live, jnp.exp(scores - reference), 0.0)
    scale = jnp.exp(m_cache - reference)
    row_sum = scale * l_ref[:, 0:1] + jnp.sum(weights, axis=1, keepdims=True)
    weighted = scale * o_ref[...] + jnp.dot(
        weights.astype(jnp.bfloat16), span_v, preferred_element_type=jnp.float32
    )
    empty = row_sum == 0.0
    shared = jnp.where(empty, 0.0, weighted / jnp.where(empty, 1.0, row_sum)).astype(jnp.bfloat16)
    sum_high = row_sum.astype(jnp.bfloat16).astype(jnp.float32)
    sum_low = row_sum - sum_high
    lane = lax.broadcasted_iota(jnp.int32, (rows, HD), 1)
    row = lax.broadcasted_iota(jnp.int32, (rows, HD), 0)
    spread = jnp.where(lane == row, reference, 0.0)
    spread = jnp.where(lane == row + rows, sum_high, spread)
    spread = jnp.where(lane == row + 2 * rows, sum_low, spread)
    stats = jnp.sum(spread, axis=0, keepdims=True)
    tail = jnp.dot(place_key_ref[...], span_k, preferred_element_type=jnp.float32)
    tail = tail + jnp.dot(place_value_ref[...], span_v, preferred_element_type=jnp.float32)
    within = lax.broadcasted_iota(jnp.int32, tail.shape, 0) % TAIL
    tail = jnp.where(within == 2 * CAP, jnp.broadcast_to(stats, tail.shape), tail)
    out_ref[:, rows:, :] = tail.astype(jnp.bfloat16).reshape(seq_count, TAIL, HD)
    for dest in range(seq_count):
        out_ref[dest, :rows, :] = shared


def span_part(parts, cache_state, seq_count):
    rows = cache_state[0].shape[0]
    return pl.pallas_call(
        span_kernel,
        in_specs=[whole()] * (1 + len(cache_state)),
        out_specs=whole(),
        out_shape=jax.ShapeDtypeStruct((seq_count, rows + TAIL, HD), jnp.bfloat16),
        compiler_params=pltpu.CompilerParams(vmem_limit_bytes=8 * MIB),
        name="span_part",
    )(parts, *cache_state)


def out_kernel(
    requests, message_ref, weight_ref, out_ref, key_hbm, value_hbm, key_ref, value_ref, sems
):
    seq_count = message_ref.shape[0]
    rows = message_ref.shape[1] - TAIL
    per_group = rows // requests
    tails = message_ref[:, rows:, :]
    key_ref[...] = tails[:, :CAP].reshape(key_ref.shape)
    value_ref[...] = tails[:, CAP : 2 * CAP].reshape(value_ref.shape)
    copies = [
        pltpu.make_async_copy(key_ref, key_hbm, sems.at[0]),
        pltpu.make_async_copy(value_ref, value_hbm, sems.at[1]),
    ]
    for copy in copies:
        copy.start()
    tails = tails.astype(jnp.float32)
    within = lax.broadcasted_iota(jnp.int32, tails.shape, 1)
    stats = jnp.sum(jnp.where(within == 2 * CAP, tails, 0.0), axis=1)
    m = stats[:, :rows]
    sums = stats[:, rows : 2 * rows] + stats[:, 2 * rows : 3 * rows]
    share = jnp.exp(m - jnp.max(m, axis=0, keepdims=True)) * sums
    share = share / jnp.sum(share, axis=0, keepdims=True)
    share = share.T
    total = jnp.zeros((rows, HD), jnp.float32)
    for source in range(seq_count):
        total = total + share[:, source : source + 1] * message_ref[source, :rows, :].astype(
            jnp.float32
        )
    attended = jnp.concatenate(
        [total[h * requests : (h + 1) * requests] for h in range(per_group)], axis=1
    ).astype(jnp.bfloat16)
    projected = jnp.dot(attended, weight_ref[...], preferred_element_type=jnp.float32)
    for dest in range(out_ref.shape[0]):
        out_ref[dest] = projected
    for copy in copies:
        copy.wait()


def out_part(messages, out_weight, requests, tp_count):
    slots = jax.ShapeDtypeStruct((messages.shape[0] * CAP, HD), jnp.bfloat16)
    return pl.pallas_call(
        functools.partial(out_kernel, requests),
        in_specs=[whole()] * 2,
        out_specs=[whole(), whole(pltpu.HBM), whole(pltpu.HBM)],
        out_shape=[
            jax.ShapeDtypeStruct((tp_count, requests, out_weight.shape[1]), jnp.float32),
            slots,
            slots,
        ],
        scratch_shapes=[
            VMEM(slots.shape, slots.dtype),
            VMEM(slots.shape, slots.dtype),
            pltpu.SemaphoreType.DMA((2,)),
        ],
        compiler_params=pltpu.CompilerParams(vmem_limit_bytes=8 * MIB),
        name="out_part",
    )(messages, out_weight)


def per_device(
    decode_query,
    cache_keys,
    cache_values,
    cache_len,
    prefill_rows,
    key_weight,
    value_weight,
    span_request,
    span_target,
    out_weight,
):
    seq_count = lax.axis_size("seq")
    tp_count = lax.axis_size("tp")
    requests = cache_keys.shape[0]
    rows = requests * decode_query.shape[1] // HD
    pre_dev = prefill_rows.shape[0] // seq_count

    own, *sent = project(prefill_rows, key_weight, value_weight)
    seq = [(y, z) for y in range(NY) for z in range(NZ)]
    came = [
        lax.ppermute(part, "seq", [(y * NZ + z, (y + k) % NY * NZ + z) for y, z in seq])
        for k, part in zip(Y_STEPS, sent)
    ]
    targets = span_target.T
    request_ids = span_request.reshape(targets.shape)
    cache_state = cache_part(
        cache_len, decode_query, cache_keys, cache_values, targets, request_ids, seq_count
    )
    partial = fold(cache_state[0], [own, *came]).reshape(NZ, pre_dev, 2 * HD)
    parts = lax.all_to_all(
        partial,
        "seq",
        split_axis=0,
        concat_axis=0,
        tiled=True,
        axis_index_groups=[[y * NZ + z for z in range(NZ)] for y in range(NY)],
    )
    outgoing = span_part(parts, cache_state, seq_count)
    messages = lax.all_to_all(outgoing, "seq", split_axis=0, concat_axis=0, tiled=True)
    shares, appended_keys, appended_values = out_part(
        messages, out_weight, requests, tp_count
    )
    shares = lax.all_to_all(shares, "tp", split_axis=0, concat_axis=0, tiled=True)
    layer_out = jnp.sum(shares, axis=0).astype(jnp.bfloat16)
    return (layer_out, appended_keys, appended_values)


def solution(mesh):
    placed = (
        P(None, "tp"),
        P(None, "seq", "tp"),
        P(None, "seq", "tp"),
        P(),
        P(None, "seq"),
        P("seq", "tp"),
        P("seq", "tp"),
        P(),
        P(),
        P("tp", "seq"),
    )
    return jax.shard_map(
        per_device,
        mesh=mesh,
        in_specs=placed,
        out_specs=(P(None, "seq"), P("seq", "tp"), P("seq", "tp")),
        check_vma=False,
    )
```

```python
import functools

import jax
import jax.numpy as jnp
from jax import lax
from jax.experimental import pallas as pl
from jax.experimental.pallas import tpu as pltpu
from jax.sharding import PartitionSpec as P

H = 64
KVH = 8
HD = 128
CAP = 2
DEAD = -(2.0**100)
NY = 4
NZ = 8
Y_STEPS = (1, 3, 2)
TAIL = 8
VMEM = pltpu.VMEM
SMEM = pltpu.SMEM
MIB = 1 << 20


def whole(space=VMEM):
    return pl.BlockSpec(memory_space=space)


def in_hbm(array):
    return pltpu.with_memory_space_constraint(array, pltpu.HBM)


def project_kernel(
    rows_hbm, key_hbm, value_hbm, own_ref, to1_ref, to2_ref, to3_ref, rows_ref, weight_ref, sems
):
    copies = [
        pltpu.make_async_copy(key_hbm, weight_ref.at[:, :HD], sems.at[0]),
        pltpu.make_async_copy(value_hbm, weight_ref.at[:, HD:], sems.at[1]),
        pltpu.make_async_copy(rows_hbm, rows_ref, sems.at[2]),
    ]
    for copy in copies:
        copy.start()
    for copy in copies:
        copy.wait()
    weight = weight_ref[...]
    y = lax.axis_index("seq") // NZ
    size = own_ref.shape[0]
    for k, ref in zip((0,) + Y_STEPS, (own_ref, to1_ref, to2_ref, to3_ref)):
        first = pl.multiple_of(lax.rem(y + k, NY) * size, size)
        ref[...] = jnp.dot(
            rows_ref[pl.ds(first, size), :], weight, preferred_element_type=jnp.float32
        ).astype(jnp.bfloat16)


def project(rows, key_weight, value_weight):
    tokens, features = rows.shape
    return pl.pallas_call(
        project_kernel,
        in_specs=[whole(pltpu.HBM)] * 3,
        out_specs=[whole()] * NY,
        out_shape=[jax.ShapeDtypeStruct((tokens // NY, 2 * HD), jnp.bfloat16)] * NY,
        scratch_shapes=[
            VMEM((tokens, features), jnp.bfloat16),
            VMEM((features, 2 * HD), jnp.bfloat16),
            pltpu.SemaphoreType.DMA((3,)),
        ],
        compiler_params=pltpu.CompilerParams(vmem_limit_bytes=8 * MIB),
        name="project",
    )(in_hbm(rows), in_hbm(key_weight), in_hbm(value_weight))


def fold_kernel(after_ref, own_ref, from1_ref, from2_ref, from3_ref, out_ref):
    total = own_ref[...].astype(jnp.float32)
    for ref in (from1_ref, from2_ref, from3_ref):
        total = total + ref[...].astype(jnp.float32)
    out_ref[...] = total.astype(jnp.bfloat16)


def fold(after, parts):
    return pl.pallas_call(
        fold_kernel,
        in_specs=[whole()] * 5,
        out_specs=whole(),
        out_shape=jax.ShapeDtypeStruct(parts[0].shape, jnp.bfloat16),
        compiler_params=pltpu.CompilerParams(vmem_limit_bytes=8 * MIB),
        name="fold",
    )(after, *parts)


def stacked_queries(query_ref, per_group):
    query = query_ref[...]
    return jnp.concatenate(
        [query[:, h * HD : (h + 1) * HD] for h in range(per_group)], axis=0
    )


def cache_kernel(
    requests,
    per_group,
    len_hbm,
    query_hbm,
    target_hbm,
    request_hbm,
    keys_hbm,
    values_hbm,
    o_ref,
    m_ref,
    l_ref,
    place_key_ref,
    place_value_ref,
    live_ref,
    stacked_ref,
    len_ref,
    query_ref,
    target_ref,
    request_ref,
    keys_ref,
    values_ref,
    query_rows,
    o_rows,
    m_rows,
    l_rows,
    small_sems,
    sems,
):
    seq_index = lax.axis_index("seq")
    rows = requests * per_group
    local_len = keys_ref.shape[1]
    tokens = live_ref.shape[1]
    small = [
        pltpu.make_async_copy(source, dest, small_sems.at[i])
        for i, (source, dest) in enumerate(
            (
                (len_hbm, len_ref),
                (query_hbm, query_ref),
                (target_hbm, target_ref),
                (request_hbm, request_ref),
            )
        )
    ]
    key_copies = [
        pltpu.make_async_copy(keys_hbm.at[r], keys_ref.at[r], sems.at[0, r])
        for r in range(requests)
    ]
    value_copies = [
        pltpu.make_async_copy(values_hbm.at[r], values_ref.at[r], sems.at[1, r])
        for r in range(requests)
    ]
    for copy in small:
        copy.start()
    for r in range(requests):
        key_copies[r].start()
        value_copies[r].start()
    for copy in small:
        copy.wait()

    per_tile = HD // tokens
    first = pl.multiple_of(seq_index // per_tile * HD, HD)
    shift = lax.rem(HD - lax.rem(seq_index, per_tile) * tokens, HD)

    def own(ref):
        tile = jnp.broadcast_to(ref[:, pl.ds(first, HD)], (8, HD))
        return pltpu.roll(tile, shift, 1)[0:1, :tokens]

    target_row = own(target_ref)
    target = jnp.broadcast_to(target_row, (tokens, tokens))
    i = lax.broadcasted_iota(jnp.int32, (tokens, tokens), 0)
    j = lax.broadcasted_iota(jnp.int32, (tokens, tokens), 1)
    column = jnp.sum(jnp.where(i == j, target, 0), axis=1, keepdims=True)
    rank = jnp.sum(jnp.where((column == target) & (i < j), 1, 0), axis=0, keepdims=True)
    slot = target_row * CAP + rank
    count = place_key_ref.shape[0]
    row = lax.broadcasted_iota(jnp.int32, (count, tokens), 0)
    dest, within = row // TAIL, row % TAIL
    wanted = jnp.broadcast_to(slot, (count, tokens))
    is_key = (within < CAP) & (wanted == dest * CAP + within)
    is_value = (within >= CAP) & (within < 2 * CAP) & (wanted == dest * CAP + within - CAP)
    place_key_ref[...] = jnp.where(is_key, 1.0, 0.0).astype(jnp.bfloat16)
    place_value_ref[...] = jnp.where(is_value, 1.0, 0.0).astype(jnp.bfloat16)
    owner = jnp.broadcast_to(own(request_ref), (rows, tokens))
    mine = lax.broadcasted_iota(jnp.int32, (rows, tokens), 0) % requests
    live_ref[...] = jnp.where(owner == mine, 1.0, 0.0)

    stacked = stacked_queries(query_ref, per_group)
    stacked_ref[...] = stacked
    query_rows[...] = stacked.astype(jnp.float32)
    for r in range(requests):
        query = query_rows[pl.ds(r, per_group, stride=requests), :].astype(jnp.bfloat16)
        key_copies[r].wait()
        scores = lax.dot_general(
            query, keys_ref[r], (((1,), (1,)), ((), ())), preferred_element_type=jnp.float32
        ) * HD ** (-0.5)
        position = seq_index * local_len + lax.broadcasted_iota(jnp.int32, scores.shape, 1)
        allowed = position < len_ref[r]
        scores = jnp.where(allowed, scores, DEAD)
        top = jnp.max(scores, axis=1, keepdims=True)
        weights = jnp.where(allowed, jnp.exp(scores - top), 0.0)
        own_rows = pl.ds(r * per_group, per_group)
        l_rows[own_rows, :] = jnp.broadcast_to(
            jnp.sum(weights, axis=1, keepdims=True), (per_group, HD)
        )
        m_rows[own_rows, :] = jnp.broadcast_to(top, (per_group, HD))
        value_copies[r].wait()
        o_rows[own_rows, :] = jnp.dot(
            weights.astype(jnp.bfloat16), values_ref[r], preferred_element_type=jnp.float32
        )
    for h in range(per_group):
        to = pl.ds(h * requests, requests)
        of = pl.ds(h, requests, stride=per_group)
        o_ref[to, :] = o_rows[of, :]
        m_ref[to, :] = m_rows[of, :]
        l_ref[to, :] = l_rows[of, :]


def cache_part(cache_len, query, keys, values, target, request_ids, seq_count):
    requests, local_len, _ = keys.shape
    per_group = query.shape[1] // HD
    rows = requests * per_group
    tokens = target.shape[1] // seq_count
    f32 = jnp.float32
    table = jax.ShapeDtypeStruct((rows, HD), f32)
    place = jax.ShapeDtypeStruct((seq_count * TAIL, tokens), jnp.bfloat16)
    operands = (cache_len, query, target, request_ids, keys, values)
    return pl.pallas_call(
        functools.partial(cache_kernel, requests, per_group),
        in_specs=[whole(pltpu.HBM)] * 6,
        out_specs=[whole()] * 7,
        out_shape=[
            table,
            table,
            table,
            place,
            place,
            jax.ShapeDtypeStruct((rows, tokens), f32),
            jax.ShapeDtypeStruct((rows, HD), query.dtype),
        ],
        scratch_shapes=[SMEM(cache_len.shape, cache_len.dtype)]
        + [VMEM(a.shape, a.dtype) for a in operands[1:]]
        + [VMEM((rows, HD), f32)] * 4
        + [pltpu.SemaphoreType.DMA((4,)), pltpu.SemaphoreType.DMA((2, requests))],
        cost_estimate=pl.CostEstimate(
            flops=4 * rows * local_len * HD,
            bytes_accessed=4 * requests * local_len * HD,
            transcendentals=rows * local_len,
        ),
        compiler_params=pltpu.CompilerParams(vmem_limit_bytes=16 * MIB),
        name="cache_part",
    )(*[in_hbm(a) for a in operands])


def span_kernel(
    parts_ref,
    o_ref,
    m_ref,
    l_ref,
    place_key_ref,
    place_value_ref,
    live_ref,
    query_ref,
    out_ref,
):
    rows = o_ref.shape[0]
    seq_count = out_ref.shape[0]
    total = parts_ref[0].astype(jnp.float32)
    for source in range(1, parts_ref.shape[0]):
        total = total + parts_ref[source].astype(jnp.float32)
    owned = total.astype(jnp.bfloat16)
    span_k, span_v = owned[:, :HD], owned[:, HD:]
    live = live_ref[...] > 0.5
    scores = lax.dot_general(
        query_ref[...], span_k, (((1,), (1,)), ((), ())), preferred_element_type=jnp.float32
    ) * HD ** (-0.5)
    scores = jnp.where(live, scores, DEAD)
    m_cache = m_ref[:, 0:1]
    reference = (
        jnp.maximum(m_cache, jnp.max(scores, axis=1, keepdims=True))
        .astype(jnp.bfloat16)
        .astype(jnp.float32)
    )
    weights = jnp.where(live, jnp.exp(scores - reference), 0.0)
    scale = jnp.exp(m_cache - reference)
    row_sum = scale * l_ref[:, 0:1] + jnp.sum(weights, axis=1, keepdims=True)
    weighted = scale * o_ref[...] + jnp.dot(
        weights.astype(jnp.bfloat16), span_v, preferred_element_type=jnp.float32
    )
    empty = row_sum == 0.0
    shared = jnp.where(empty, 0.0, weighted / jnp.where(empty, 1.0, row_sum)).astype(jnp.bfloat16)
    sum_high = row_sum.astype(jnp.bfloat16).astype(jnp.float32)
    sum_low = row_sum - sum_high
    lane = lax.broadcasted_iota(jnp.int32, (rows, HD), 1)
    row = lax.broadcasted_iota(jnp.int32, (rows, HD), 0)
    spread = jnp.where(lane == row, reference, 0.0)
    spread = jnp.where(lane == row + rows, sum_high, spread)
    spread = jnp.where(lane == row + 2 * rows, sum_low, spread)
    stats = jnp.sum(spread, axis=0, keepdims=True)
    tail = jnp.dot(place_key_ref[...], span_k, preferred_element_type=jnp.float32)
    tail = tail + jnp.dot(place_value_ref[...], span_v, preferred_element_type=jnp.float32)
    within = lax.broadcasted_iota(jnp.int32, tail.shape, 0) % TAIL
    tail = jnp.where(within == 2 * CAP, jnp.broadcast_to(stats, tail.shape), tail)
    out_ref[:, rows:, :] = tail.astype(jnp.bfloat16).reshape(seq_count, TAIL, HD)
    for dest in range(seq_count):
        out_ref[dest, :rows, :] = shared


def span_part(parts, cache_state, seq_count):
    rows = cache_state[0].shape[0]
    return pl.pallas_call(
        span_kernel,
        in_specs=[whole()] * (1 + len(cache_state)),
        out_specs=whole(),
        out_shape=jax.ShapeDtypeStruct((seq_count, rows + TAIL, HD), jnp.bfloat16),
        compiler_params=pltpu.CompilerParams(vmem_limit_bytes=8 * MIB),
        name="span_part",
    )(parts, *cache_state)


def out_kernel(requests, message_ref, weight_ref, out_ref):
    seq_count = message_ref.shape[0]
    rows = message_ref.shape[1] - TAIL
    per_group = rows // requests
    tails = message_ref[:, rows:, :].astype(jnp.float32)
    within = lax.broadcasted_iota(jnp.int32, tails.shape, 1)
    stats = jnp.sum(jnp.where(within == 2 * CAP, tails, 0.0), axis=1)
    m = stats[:, :rows]
    sums = stats[:, rows : 2 * rows] + stats[:, 2 * rows : 3 * rows]
    share = jnp.exp(m - jnp.max(m, axis=0, keepdims=True)) * sums
    share = share / jnp.sum(share, axis=0, keepdims=True)
    share = share.T
    total = jnp.zeros((rows, HD), jnp.float32)
    for source in range(seq_count):
        total = total + share[:, source : source + 1] * message_ref[source, :rows, :].astype(
            jnp.float32
        )
    attended = jnp.concatenate(
        [total[h * requests : (h + 1) * requests] for h in range(per_group)], axis=1
    ).astype(jnp.bfloat16)
    projected = jnp.dot(attended, weight_ref[...], preferred_element_type=jnp.float32)
    for dest in range(out_ref.shape[0]):
        out_ref[dest] = projected


def out_part(messages, out_weight, requests, tp_count):
    return pl.pallas_call(
        functools.partial(out_kernel, requests),
        in_specs=[whole()] * 2,
        out_specs=whole(),
        out_shape=jax.ShapeDtypeStruct((tp_count, requests, out_weight.shape[1]), jnp.float32),
        compiler_params=pltpu.CompilerParams(vmem_limit_bytes=8 * MIB),
        name="out_part",
    )(messages, out_weight)


def finish_kernel(
    message_ref, share_ref, out_hbm, key_hbm, value_hbm, out_ref, key_ref, value_ref, sems
):
    rows = message_ref.shape[1] - TAIL
    tails = message_ref[:, rows:, :]
    key_ref[...] = tails[:, :CAP].reshape(key_ref.shape)
    value_ref[...] = tails[:, CAP : 2 * CAP].reshape(value_ref.shape)
    copies = [
        pltpu.make_async_copy(source, dest, sems.at[i])
        for i, (source, dest) in enumerate(
            ((out_ref, out_hbm), (key_ref, key_hbm), (value_ref, value_hbm))
        )
    ]
    copies[1].start()
    copies[2].start()
    out_ref[...] = jnp.sum(share_ref[...], axis=0).astype(jnp.bfloat16)
    copies[0].start()
    for copy in copies:
        copy.wait()


def finish(messages, shares):
    slots = jax.ShapeDtypeStruct((messages.shape[0] * CAP, HD), jnp.bfloat16)
    outs = [jax.ShapeDtypeStruct(shares.shape[1:], jnp.bfloat16), slots, slots]
    return pl.pallas_call(
        finish_kernel,
        in_specs=[whole()] * 2,
        out_specs=[whole(pltpu.HBM)] * 3,
        out_shape=outs,
        scratch_shapes=[VMEM(a.shape, a.dtype) for a in outs] + [pltpu.SemaphoreType.DMA((3,))],
        compiler_params=pltpu.CompilerParams(vmem_limit_bytes=8 * MIB),
        name="finish",
    )(messages, shares)


def per_device(
    decode_query,
    cache_keys,
    cache_values,
    cache_len,
    prefill_rows,
    key_weight,
    value_weight,
    span_request,
    span_target,
    out_weight,
):
    seq_count = lax.axis_size("seq")
    tp_count = lax.axis_size("tp")
    requests = cache_keys.shape[0]
    rows = requests * decode_query.shape[1] // HD
    pre_dev = prefill_rows.shape[0] // seq_count

    own, *sent = project(prefill_rows, key_weight, value_weight)
    seq = [(y, z) for y in range(NY) for z in range(NZ)]
    came = [
        lax.ppermute(part, "seq", [(y * NZ + z, (y + k) % NY * NZ + z) for y, z in seq])
        for k, part in zip(Y_STEPS, sent)
    ]
    targets = span_target.T
    request_ids = span_request.reshape(targets.shape)
    cache_state = cache_part(
        cache_len, decode_query, cache_keys, cache_values, targets, request_ids, seq_count
    )
    partial = fold(cache_state[0], [own, *came]).reshape(NZ, pre_dev, 2 * HD)
    parts = lax.all_to_all(
        partial,
        "seq",
        split_axis=0,
        concat_axis=0,
        tiled=True,
        axis_index_groups=[[y * NZ + z for z in range(NZ)] for y in range(NY)],
    )
    outgoing = span_part(parts, cache_state, seq_count)
    messages = lax.all_to_all(outgoing, "seq", split_axis=0, concat_axis=0, tiled=True)
    shares = out_part(messages, out_weight, requests, tp_count)
    shares = lax.all_to_all(shares, "tp", split_axis=0, concat_axis=0, tiled=True)
    return finish(messages, shares)


def solution(mesh):
    placed = (
        P(None, "tp"),
        P(None, "seq", "tp"),
        P(None, "seq", "tp"),
        P(),
        P(None, "seq"),
        P("seq", "tp"),
        P("seq", "tp"),
        P(),
        P(),
        P("tp", "seq"),
    )
    return jax.shard_map(
        per_device,
        mesh=mesh,
        in_specs=placed,
        out_specs=(P(None, "seq"), P("seq", "tp"), P("seq", "tp")),
        check_vma=False,
    )
```

```python
import functools

import jax
import jax.numpy as jnp
from jax import lax
from jax.experimental import pallas as pl
from jax.experimental.pallas import tpu as pltpu
from jax.sharding import PartitionSpec as P

H = 64
KVH = 8
HD = 128
CAP = 2
DEAD = -(2.0**100)
NY = 4
NZ = 8
Y_STEPS = (1, 3, 2)
TAIL = 8
VMEM = pltpu.VMEM
SMEM = pltpu.SMEM
MIB = 1 << 20


def whole(space=VMEM):
    return pl.BlockSpec(memory_space=space)


def in_hbm(array):
    return pltpu.with_memory_space_constraint(array, pltpu.HBM)


def project_kernel(
    rows_hbm, key_hbm, value_hbm, own_ref, to1_ref, to2_ref, to3_ref, rows_ref, weight_ref, sems
):
    copies = [
        pltpu.make_async_copy(key_hbm, weight_ref.at[:, :HD], sems.at[0]),
        pltpu.make_async_copy(value_hbm, weight_ref.at[:, HD:], sems.at[1]),
        pltpu.make_async_copy(rows_hbm, rows_ref, sems.at[2]),
    ]
    for copy in copies:
        copy.start()
    for copy in copies:
        copy.wait()
    weight = weight_ref[...]
    y = lax.axis_index("seq") // NZ
    size = own_ref.shape[0]
    for k, ref in zip((0,) + Y_STEPS, (own_ref, to1_ref, to2_ref, to3_ref)):
        first = pl.multiple_of(lax.rem(y + k, NY) * size, size)
        ref[...] = jnp.dot(
            rows_ref[pl.ds(first, size), :], weight, preferred_element_type=jnp.float32
        ).astype(jnp.bfloat16)


def project(rows, key_weight, value_weight):
    tokens, features = rows.shape
    return pl.pallas_call(
        project_kernel,
        in_specs=[whole(pltpu.HBM)] * 3,
        out_specs=[whole()] * NY,
        out_shape=[jax.ShapeDtypeStruct((tokens // NY, 2 * HD), jnp.bfloat16)] * NY,
        scratch_shapes=[
            VMEM((tokens, features), jnp.bfloat16),
            VMEM((features, 2 * HD), jnp.bfloat16),
            pltpu.SemaphoreType.DMA((3,)),
        ],
        compiler_params=pltpu.CompilerParams(vmem_limit_bytes=8 * MIB),
        name="project",
    )(in_hbm(rows), in_hbm(key_weight), in_hbm(value_weight))


def fold_kernel(after_ref, own_ref, from1_ref, from2_ref, from3_ref, out_ref):
    total = own_ref[...].astype(jnp.float32)
    for ref in (from1_ref, from2_ref, from3_ref):
        total = total + ref[...].astype(jnp.float32)
    total = total.astype(jnp.bfloat16)
    size = total.shape[0] // NZ
    for z in range(NZ):
        place = (NZ - 1 - z) * size
        out_ref[place : place + size, :] = total[z * size : (z + 1) * size]


def fold(after, parts):
    return pl.pallas_call(
        fold_kernel,
        in_specs=[whole()] * 5,
        out_specs=whole(),
        out_shape=jax.ShapeDtypeStruct(parts[0].shape, jnp.bfloat16),
        compiler_params=pltpu.CompilerParams(vmem_limit_bytes=8 * MIB),
        name="fold",
    )(after, *parts)


def stacked_queries(query_ref, per_group):
    query = query_ref[...]
    return jnp.concatenate(
        [query[:, h * HD : (h + 1) * HD] for h in range(per_group)], axis=0
    )


def cache_kernel(
    requests,
    per_group,
    len_hbm,
    query_hbm,
    target_hbm,
    request_hbm,
    keys_hbm,
    values_hbm,
    o_ref,
    m_ref,
    l_ref,
    place_key_ref,
    place_value_ref,
    live_ref,
    stacked_ref,
    len_ref,
    query_ref,
    target_ref,
    request_ref,
    keys_ref,
    values_ref,
    query_rows,
    o_rows,
    m_rows,
    l_rows,
    small_sems,
    sems,
):
    seq_index = lax.axis_index("seq")
    rows = requests * per_group
    local_len = keys_ref.shape[1]
    tokens = live_ref.shape[1]
    small = [
        pltpu.make_async_copy(source, dest, small_sems.at[i])
        for i, (source, dest) in enumerate(
            (
                (len_hbm, len_ref),
                (query_hbm, query_ref),
                (target_hbm, target_ref),
                (request_hbm, request_ref),
            )
        )
    ]
    key_copies = [
        pltpu.make_async_copy(keys_hbm.at[r], keys_ref.at[r], sems.at[0, r])
        for r in range(requests)
    ]
    value_copies = [
        pltpu.make_async_copy(values_hbm.at[r], values_ref.at[r], sems.at[1, r])
        for r in range(requests)
    ]
    for copy in small:
        copy.start()
    for r in range(requests):
        key_copies[r].start()
        value_copies[r].start()
    for copy in small:
        copy.wait()

    per_tile = HD // tokens
    first = pl.multiple_of(seq_index // per_tile * HD, HD)
    shift = lax.rem(HD - lax.rem(seq_index, per_tile) * tokens, HD)

    def own(ref):
        tile = jnp.broadcast_to(ref[:, pl.ds(first, HD)], (8, HD))
        return pltpu.roll(tile, shift, 1)[0:1, :tokens]

    target_row = own(target_ref)
    target = jnp.broadcast_to(target_row, (tokens, tokens))
    i = lax.broadcasted_iota(jnp.int32, (tokens, tokens), 0)
    j = lax.broadcasted_iota(jnp.int32, (tokens, tokens), 1)
    column = jnp.sum(jnp.where(i == j, target, 0), axis=1, keepdims=True)
    rank = jnp.sum(jnp.where((column == target) & (i < j), 1, 0), axis=0, keepdims=True)
    slot = target_row * CAP + rank
    count = place_key_ref.shape[0]
    row = lax.broadcasted_iota(jnp.int32, (count, tokens), 0)
    dest, within = count // TAIL - 1 - row // TAIL, row % TAIL
    wanted = jnp.broadcast_to(slot, (count, tokens))
    is_key = (within < CAP) & (wanted == dest * CAP + within)
    is_value = (within >= CAP) & (within < 2 * CAP) & (wanted == dest * CAP + within - CAP)
    place_key_ref[...] = jnp.where(is_key, 1.0, 0.0).astype(jnp.bfloat16)
    place_value_ref[...] = jnp.where(is_value, 1.0, 0.0).astype(jnp.bfloat16)
    owner = jnp.broadcast_to(own(request_ref), (rows, tokens))
    mine = lax.broadcasted_iota(jnp.int32, (rows, tokens), 0) % requests
    live_ref[...] = jnp.where(owner == mine, 1.0, 0.0)

    stacked = stacked_queries(query_ref, per_group)
    stacked_ref[...] = stacked
    query_rows[...] = stacked.astype(jnp.float32)
    for r in range(requests):
        query = query_rows[pl.ds(r, per_group, stride=requests), :].astype(jnp.bfloat16)
        key_copies[r].wait()
        scores = lax.dot_general(
            query, keys_ref[r], (((1,), (1,)), ((), ())), preferred_element_type=jnp.float32
        ) * HD ** (-0.5)
        position = seq_index * local_len + lax.broadcasted_iota(jnp.int32, scores.shape, 1)
        allowed = position < len_ref[r]
        scores = jnp.where(allowed, scores, DEAD)
        top = jnp.max(scores, axis=1, keepdims=True)
        weights = jnp.where(allowed, jnp.exp(scores - top), 0.0)
        own_rows = pl.ds(r * per_group, per_group)
        l_rows[own_rows, :] = jnp.broadcast_to(
            jnp.sum(weights, axis=1, keepdims=True), (per_group, HD)
        )
        m_rows[own_rows, :] = jnp.broadcast_to(top, (per_group, HD))
        value_copies[r].wait()
        o_rows[own_rows, :] = jnp.dot(
            weights.astype(jnp.bfloat16), values_ref[r], preferred_element_type=jnp.float32
        )
    for h in range(per_group):
        to = pl.ds(h * requests, requests)
        of = pl.ds(h, requests, stride=per_group)
        o_ref[to, :] = o_rows[of, :]
        m_ref[to, :] = m_rows[of, :]
        l_ref[to, :] = l_rows[of, :]


def cache_part(cache_len, query, keys, values, target, request_ids, seq_count):
    requests, local_len, _ = keys.shape
    per_group = query.shape[1] // HD
    rows = requests * per_group
    tokens = target.shape[1] // seq_count
    f32 = jnp.float32
    table = jax.ShapeDtypeStruct((rows, HD), f32)
    place = jax.ShapeDtypeStruct((seq_count * TAIL, tokens), jnp.bfloat16)
    operands = (cache_len, query, target, request_ids, keys, values)
    return pl.pallas_call(
        functools.partial(cache_kernel, requests, per_group),
        in_specs=[whole(pltpu.HBM)] * 6,
        out_specs=[whole()] * 7,
        out_shape=[
            table,
            table,
            table,
            place,
            place,
            jax.ShapeDtypeStruct((rows, tokens), f32),
            jax.ShapeDtypeStruct((rows, HD), query.dtype),
        ],
        scratch_shapes=[SMEM(cache_len.shape, cache_len.dtype)]
        + [VMEM(a.shape, a.dtype) for a in operands[1:]]
        + [VMEM((rows, HD), f32)] * 4
        + [pltpu.SemaphoreType.DMA((4,)), pltpu.SemaphoreType.DMA((2, requests))],
        cost_estimate=pl.CostEstimate(
            flops=4 * rows * local_len * HD,
            bytes_accessed=4 * requests * local_len * HD,
            transcendentals=rows * local_len,
        ),
        compiler_params=pltpu.CompilerParams(vmem_limit_bytes=16 * MIB),
        name="cache_part",
    )(*[in_hbm(a) for a in operands])


def span_kernel(
    parts_ref,
    o_ref,
    m_ref,
    l_ref,
    place_key_ref,
    place_value_ref,
    live_ref,
    query_ref,
    out_ref,
):
    rows = o_ref.shape[0]
    seq_count = out_ref.shape[0]
    total = parts_ref[0].astype(jnp.float32)
    for source in range(1, parts_ref.shape[0]):
        total = total + parts_ref[source].astype(jnp.float32)
    owned = total.astype(jnp.bfloat16)
    span_k, span_v = owned[:, :HD], owned[:, HD:]
    live = live_ref[...] > 0.5
    scores = lax.dot_general(
        query_ref[...], span_k, (((1,), (1,)), ((), ())), preferred_element_type=jnp.float32
    ) * HD ** (-0.5)
    scores = jnp.where(live, scores, DEAD)
    m_cache = m_ref[:, 0:1]
    reference = (
        jnp.maximum(m_cache, jnp.max(scores, axis=1, keepdims=True))
        .astype(jnp.bfloat16)
        .astype(jnp.float32)
    )
    weights = jnp.where(live, jnp.exp(scores - reference), 0.0)
    scale = jnp.exp(m_cache - reference)
    row_sum = scale * l_ref[:, 0:1] + jnp.sum(weights, axis=1, keepdims=True)
    weighted = scale * o_ref[...] + jnp.dot(
        weights.astype(jnp.bfloat16), span_v, preferred_element_type=jnp.float32
    )
    empty = row_sum == 0.0
    shared = jnp.where(empty, 0.0, weighted / jnp.where(empty, 1.0, row_sum)).astype(jnp.bfloat16)
    sum_high = row_sum.astype(jnp.bfloat16).astype(jnp.float32)
    sum_low = row_sum - sum_high
    lane = lax.broadcasted_iota(jnp.int32, (rows, HD), 1)
    row = lax.broadcasted_iota(jnp.int32, (rows, HD), 0)
    spread = jnp.where(lane == row, reference, 0.0)
    spread = jnp.where(lane == row + rows, sum_high, spread)
    spread = jnp.where(lane == row + 2 * rows, sum_low, spread)
    stats = jnp.sum(spread, axis=0, keepdims=True)
    tail = jnp.dot(place_key_ref[...], span_k, preferred_element_type=jnp.float32)
    tail = tail + jnp.dot(place_value_ref[...], span_v, preferred_element_type=jnp.float32)
    within = lax.broadcasted_iota(jnp.int32, tail.shape, 0) % TAIL
    tail = jnp.where(within == 2 * CAP, jnp.broadcast_to(stats, tail.shape), tail)
    out_ref[:, rows:, :] = tail.astype(jnp.bfloat16).reshape(seq_count, TAIL, HD)
    for dest in range(seq_count):
        out_ref[dest, :rows, :] = shared


def span_part(parts, cache_state, seq_count):
    rows = cache_state[0].shape[0]
    return pl.pallas_call(
        span_kernel,
        in_specs=[whole()] * (1 + len(cache_state)),
        out_specs=whole(),
        out_shape=jax.ShapeDtypeStruct((seq_count, rows + TAIL, HD), jnp.bfloat16),
        compiler_params=pltpu.CompilerParams(vmem_limit_bytes=8 * MIB),
        name="span_part",
    )(parts, *cache_state)


def out_kernel(requests, message_ref, weight_ref, out_ref):
    seq_count = message_ref.shape[0]
    rows = message_ref.shape[1] - TAIL
    per_group = rows // requests
    tails = message_ref[:, rows:, :].astype(jnp.float32)
    within = lax.broadcasted_iota(jnp.int32, tails.shape, 1)
    stats = jnp.sum(jnp.where(within == 2 * CAP, tails, 0.0), axis=1)
    m = stats[:, :rows]
    sums = stats[:, rows : 2 * rows] + stats[:, 2 * rows : 3 * rows]
    share = jnp.exp(m - jnp.max(m, axis=0, keepdims=True)) * sums
    share = share / jnp.sum(share, axis=0, keepdims=True)
    share = share.T
    total = jnp.zeros((rows, HD), jnp.float32)
    for source in range(seq_count):
        total = total + share[:, source : source + 1] * message_ref[source, :rows, :].astype(
            jnp.float32
        )
    attended = jnp.concatenate(
        [total[h * requests : (h + 1) * requests] for h in range(per_group)], axis=1
    ).astype(jnp.bfloat16)
    projected = jnp.dot(attended, weight_ref[...], preferred_element_type=jnp.float32)
    for dest in range(out_ref.shape[0]):
        out_ref[dest] = projected


def out_part(messages, out_weight, requests, tp_count):
    return pl.pallas_call(
        functools.partial(out_kernel, requests),
        in_specs=[whole()] * 2,
        out_specs=whole(),
        out_shape=jax.ShapeDtypeStruct((tp_count, requests, out_weight.shape[1]), jnp.float32),
        compiler_params=pltpu.CompilerParams(vmem_limit_bytes=8 * MIB),
        name="out_part",
    )(messages, out_weight)


def finish_kernel(
    message_ref, share_ref, out_hbm, key_hbm, value_hbm, out_ref, key_ref, value_ref, sems
):
    rows = message_ref.shape[1] - TAIL
    tails = message_ref[:, rows:, :]
    count = tails.shape[0]
    tails = jnp.concatenate([tails[p : p + 1] for p in reversed(range(count))], axis=0)
    key_ref[...] = tails[:, :CAP].reshape(key_ref.shape)
    value_ref[...] = tails[:, CAP : 2 * CAP].reshape(value_ref.shape)
    copies = [
        pltpu.make_async_copy(source, dest, sems.at[i])
        for i, (source, dest) in enumerate(
            ((out_ref, out_hbm), (key_ref, key_hbm), (value_ref, value_hbm))
        )
    ]
    copies[1].start()
    copies[2].start()
    out_ref[...] = jnp.sum(share_ref[...], axis=0).astype(jnp.bfloat16)
    copies[0].start()
    for copy in copies:
        copy.wait()


def finish(messages, shares):
    slots = jax.ShapeDtypeStruct((messages.shape[0] * CAP, HD), jnp.bfloat16)
    outs = [jax.ShapeDtypeStruct(shares.shape[1:], jnp.bfloat16), slots, slots]
    return pl.pallas_call(
        finish_kernel,
        in_specs=[whole()] * 2,
        out_specs=[whole(pltpu.HBM)] * 3,
        out_shape=outs,
        scratch_shapes=[VMEM(a.shape, a.dtype) for a in outs] + [pltpu.SemaphoreType.DMA((3,))],
        compiler_params=pltpu.CompilerParams(vmem_limit_bytes=8 * MIB),
        name="finish",
    )(messages, shares)


def per_device(
    decode_query,
    cache_keys,
    cache_values,
    cache_len,
    prefill_rows,
    key_weight,
    value_weight,
    span_request,
    span_target,
    out_weight,
):
    seq_count = lax.axis_size("seq")
    tp_count = lax.axis_size("tp")
    requests = cache_keys.shape[0]
    rows = requests * decode_query.shape[1] // HD
    pre_dev = prefill_rows.shape[0] // seq_count

    own, *sent = project(prefill_rows, key_weight, value_weight)
    seq = [(y, z) for y in range(NY) for z in range(NZ)]
    came = [
        lax.ppermute(part, "seq", [(y * NZ + z, (y + k) % NY * NZ + z) for y, z in seq])
        for k, part in zip(Y_STEPS, sent)
    ]
    targets = span_target.T
    request_ids = span_request.reshape(targets.shape)
    cache_state = cache_part(
        cache_len, decode_query, cache_keys, cache_values, targets, request_ids, seq_count
    )
    partial = fold(cache_state[0], [own, *came]).reshape(NZ, pre_dev, 2 * HD)
    parts = lax.all_to_all(
        partial,
        "seq",
        split_axis=0,
        concat_axis=0,
        tiled=True,
        axis_index_groups=[[y * NZ + z for z in reversed(range(NZ))] for y in range(NY)],
    )
    outgoing = span_part(parts, cache_state, seq_count)
    messages = lax.all_to_all(
        outgoing,
        "seq",
        split_axis=0,
        concat_axis=0,
        tiled=True,
        axis_index_groups=[list(reversed(range(seq_count)))],
    )
    shares = out_part(messages, out_weight, requests, tp_count)
    shares = lax.all_to_all(
        shares,
        "tp",
        split_axis=0,
        concat_axis=0,
        tiled=True,
        axis_index_groups=[list(reversed(range(tp_count)))],
    )
    return finish(messages, shares)


def solution(mesh):
    placed = (
        P(None, "tp"),
        P(None, "seq", "tp"),
        P(None, "seq", "tp"),
        P(),
        P(None, "seq"),
        P("seq", "tp"),
        P("seq", "tp"),
        P(),
        P(),
        P("tp", "seq"),
    )
    return jax.shard_map(
        per_device,
        mesh=mesh,
        in_specs=placed,
        out_specs=(P(None, "seq"), P("seq", "tp"), P("seq", "tp")),
        check_vma=False,
    )
```

```python
import functools

import jax
import jax.numpy as jnp
from jax import lax
from jax.experimental import pallas as pl
from jax.experimental.pallas import tpu as pltpu
from jax.sharding import PartitionSpec as P

H = 64
KVH = 8
HD = 128
CAP = 2
DEAD = -(2.0**100)
NY = 4
NZ = 8
Y_STEPS = (1, 3, 2)
TAIL = 8
VMEM = pltpu.VMEM
SMEM = pltpu.SMEM
MIB = 1 << 20


def listed(place):
    y = (place >> 3 & 1) * 2 + (place >> 4 & 1)
    z = (place & 1) * 4 + (place >> 1 & 1) * 2 + (place >> 2 & 1)
    return NY * NZ - 1 - (y * NZ + z)


def whole(space=VMEM):
    return pl.BlockSpec(memory_space=space)


def in_hbm(array):
    return pltpu.with_memory_space_constraint(array, pltpu.HBM)


def project_kernel(
    rows_hbm, key_hbm, value_hbm, own_ref, to1_ref, to2_ref, to3_ref, rows_ref, weight_ref, sems
):
    copies = [
        pltpu.make_async_copy(key_hbm, weight_ref.at[:, :HD], sems.at[0]),
        pltpu.make_async_copy(value_hbm, weight_ref.at[:, HD:], sems.at[1]),
        pltpu.make_async_copy(rows_hbm, rows_ref, sems.at[2]),
    ]
    for copy in copies:
        copy.start()
    for copy in copies:
        copy.wait()
    weight = weight_ref[...]
    y = lax.axis_index("seq") // NZ
    size = own_ref.shape[0]
    for k, ref in zip((0,) + Y_STEPS, (own_ref, to1_ref, to2_ref, to3_ref)):
        first = pl.multiple_of(lax.rem(y + k, NY) * size, size)
        ref[...] = jnp.dot(
            rows_ref[pl.ds(first, size), :], weight, preferred_element_type=jnp.float32
        ).astype(jnp.bfloat16)


def project(rows, key_weight, value_weight):
    tokens, features = rows.shape
    return pl.pallas_call(
        project_kernel,
        in_specs=[whole(pltpu.HBM)] * 3,
        out_specs=[whole()] * NY,
        out_shape=[jax.ShapeDtypeStruct((tokens // NY, 2 * HD), jnp.bfloat16)] * NY,
        scratch_shapes=[
            VMEM((tokens, features), jnp.bfloat16),
            VMEM((features, 2 * HD), jnp.bfloat16),
            pltpu.SemaphoreType.DMA((3,)),
        ],
        compiler_params=pltpu.CompilerParams(vmem_limit_bytes=8 * MIB),
        name="project",
    )(in_hbm(rows), in_hbm(key_weight), in_hbm(value_weight))


def fold_kernel(after_ref, own_ref, from1_ref, from2_ref, from3_ref, out_ref):
    total = own_ref[...].astype(jnp.float32)
    for ref in (from1_ref, from2_ref, from3_ref):
        total = total + ref[...].astype(jnp.float32)
    total = total.astype(jnp.bfloat16)
    size = total.shape[0] // NZ
    for z in range(NZ):
        place = (NZ - 1 - z) * size
        out_ref[place : place + size, :] = total[z * size : (z + 1) * size]


def fold(after, parts):
    return pl.pallas_call(
        fold_kernel,
        in_specs=[whole()] * 5,
        out_specs=whole(),
        out_shape=jax.ShapeDtypeStruct(parts[0].shape, jnp.bfloat16),
        compiler_params=pltpu.CompilerParams(vmem_limit_bytes=8 * MIB),
        name="fold",
    )(after, *parts)


def stacked_queries(query_ref, per_group):
    query = query_ref[...]
    return jnp.concatenate(
        [query[:, h * HD : (h + 1) * HD] for h in range(per_group)], axis=0
    )


def cache_kernel(
    requests,
    per_group,
    len_hbm,
    query_hbm,
    target_hbm,
    request_hbm,
    keys_hbm,
    values_hbm,
    o_ref,
    m_ref,
    l_ref,
    place_key_ref,
    place_value_ref,
    live_ref,
    stacked_ref,
    len_ref,
    query_ref,
    target_ref,
    request_ref,
    keys_ref,
    values_ref,
    query_rows,
    o_rows,
    m_rows,
    l_rows,
    small_sems,
    sems,
):
    seq_index = lax.axis_index("seq")
    rows = requests * per_group
    local_len = keys_ref.shape[1]
    tokens = live_ref.shape[1]
    small = [
        pltpu.make_async_copy(source, dest, small_sems.at[i])
        for i, (source, dest) in enumerate(
            (
                (len_hbm, len_ref),
                (query_hbm, query_ref),
                (target_hbm, target_ref),
                (request_hbm, request_ref),
            )
        )
    ]
    key_copies = [
        pltpu.make_async_copy(keys_hbm.at[r], keys_ref.at[r], sems.at[0, r])
        for r in range(requests)
    ]
    value_copies = [
        pltpu.make_async_copy(values_hbm.at[r], values_ref.at[r], sems.at[1, r])
        for r in range(requests)
    ]
    for copy in small:
        copy.start()
    for r in range(requests):
        key_copies[r].start()
        value_copies[r].start()
    for copy in small:
        copy.wait()

    per_tile = HD // tokens
    first = pl.multiple_of(seq_index // per_tile * HD, HD)
    shift = lax.rem(HD - lax.rem(seq_index, per_tile) * tokens, HD)

    def own(ref):
        tile = jnp.broadcast_to(ref[:, pl.ds(first, HD)], (8, HD))
        return pltpu.roll(tile, shift, 1)[0:1, :tokens]

    target_row = own(target_ref)
    target = jnp.broadcast_to(target_row, (tokens, tokens))
    i = lax.broadcasted_iota(jnp.int32, (tokens, tokens), 0)
    j = lax.broadcasted_iota(jnp.int32, (tokens, tokens), 1)
    column = jnp.sum(jnp.where(i == j, target, 0), axis=1, keepdims=True)
    rank = jnp.sum(jnp.where((column == target) & (i < j), 1, 0), axis=0, keepdims=True)
    slot = target_row * CAP + rank
    count = place_key_ref.shape[0]
    row = lax.broadcasted_iota(jnp.int32, (count, tokens), 0)
    dest, within = listed(row // TAIL), row % TAIL
    wanted = jnp.broadcast_to(slot, (count, tokens))
    is_key = (within < CAP) & (wanted == dest * CAP + within)
    is_value = (within >= CAP) & (within < 2 * CAP) & (wanted == dest * CAP + within - CAP)
    place_key_ref[...] = jnp.where(is_key, 1.0, 0.0).astype(jnp.bfloat16)
    place_value_ref[...] = jnp.where(is_value, 1.0, 0.0).astype(jnp.bfloat16)
    owner = jnp.broadcast_to(own(request_ref), (rows, tokens))
    mine = lax.broadcasted_iota(jnp.int32, (rows, tokens), 0) % requests
    live_ref[...] = jnp.where(owner == mine, 1.0, 0.0)

    stacked = stacked_queries(query_ref, per_group)
    stacked_ref[...] = stacked
    query_rows[...] = stacked.astype(jnp.float32)
    for r in range(requests):
        query = query_rows[pl.ds(r, per_group, stride=requests), :].astype(jnp.bfloat16)
        key_copies[r].wait()
        scores = lax.dot_general(
            query, keys_ref[r], (((1,), (1,)), ((), ())), preferred_element_type=jnp.float32
        ) * HD ** (-0.5)
        position = seq_index * local_len + lax.broadcasted_iota(jnp.int32, scores.shape, 1)
        allowed = position < len_ref[r]
        scores = jnp.where(allowed, scores, DEAD)
        top = jnp.max(scores, axis=1, keepdims=True)
        weights = jnp.where(allowed, jnp.exp(scores - top), 0.0)
        own_rows = pl.ds(r * per_group, per_group)
        l_rows[own_rows, :] = jnp.broadcast_to(
            jnp.sum(weights, axis=1, keepdims=True), (per_group, HD)
        )
        m_rows[own_rows, :] = jnp.broadcast_to(top, (per_group, HD))
        value_copies[r].wait()
        o_rows[own_rows, :] = jnp.dot(
            weights.astype(jnp.bfloat16), values_ref[r], preferred_element_type=jnp.float32
        )
    for h in range(per_group):
        to = pl.ds(h * requests, requests)
        of = pl.ds(h, requests, stride=per_group)
        o_ref[to, :] = o_rows[of, :]
        m_ref[to, :] = m_rows[of, :]
        l_ref[to, :] = l_rows[of, :]


def cache_part(cache_len, query, keys, values, target, request_ids, seq_count):
    requests, local_len, _ = keys.shape
    per_group = query.shape[1] // HD
    rows = requests * per_group
    tokens = target.shape[1] // seq_count
    f32 = jnp.float32
    table = jax.ShapeDtypeStruct((rows, HD), f32)
    place = jax.ShapeDtypeStruct((seq_count * TAIL, tokens), jnp.bfloat16)
    operands = (cache_len, query, target, request_ids, keys, values)
    return pl.pallas_call(
        functools.partial(cache_kernel, requests, per_group),
        in_specs=[whole(pltpu.HBM)] * 6,
        out_specs=[whole()] * 7,
        out_shape=[
            table,
            table,
            table,
            place,
            place,
            jax.ShapeDtypeStruct((rows, tokens), f32),
            jax.ShapeDtypeStruct((rows, HD), query.dtype),
        ],
        scratch_shapes=[SMEM(cache_len.shape, cache_len.dtype)]
        + [VMEM(a.shape, a.dtype) for a in operands[1:]]
        + [VMEM((rows, HD), f32)] * 4
        + [pltpu.SemaphoreType.DMA((4,)), pltpu.SemaphoreType.DMA((2, requests))],
        cost_estimate=pl.CostEstimate(
            flops=4 * rows * local_len * HD,
            bytes_accessed=4 * requests * local_len * HD,
            transcendentals=rows * local_len,
        ),
        compiler_params=pltpu.CompilerParams(vmem_limit_bytes=16 * MIB),
        name="cache_part",
    )(*[in_hbm(a) for a in operands])


def span_kernel(
    parts_ref,
    o_ref,
    m_ref,
    l_ref,
    place_key_ref,
    place_value_ref,
    live_ref,
    query_ref,
    out_ref,
):
    rows = o_ref.shape[0]
    seq_count = out_ref.shape[0]
    total = parts_ref[0].astype(jnp.float32)
    for source in range(1, parts_ref.shape[0]):
        total = total + parts_ref[source].astype(jnp.float32)
    owned = total.astype(jnp.bfloat16)
    span_k, span_v = owned[:, :HD], owned[:, HD:]
    live = live_ref[...] > 0.5
    scores = lax.dot_general(
        query_ref[...], span_k, (((1,), (1,)), ((), ())), preferred_element_type=jnp.float32
    ) * HD ** (-0.5)
    scores = jnp.where(live, scores, DEAD)
    m_cache = m_ref[:, 0:1]
    reference = (
        jnp.maximum(m_cache, jnp.max(scores, axis=1, keepdims=True))
        .astype(jnp.bfloat16)
        .astype(jnp.float32)
    )
    weights = jnp.where(live, jnp.exp(scores - reference), 0.0)
    scale = jnp.exp(m_cache - reference)
    row_sum = scale * l_ref[:, 0:1] + jnp.sum(weights, axis=1, keepdims=True)
    weighted = scale * o_ref[...] + jnp.dot(
        weights.astype(jnp.bfloat16), span_v, preferred_element_type=jnp.float32
    )
    empty = row_sum == 0.0
    shared = jnp.where(empty, 0.0, weighted / jnp.where(empty, 1.0, row_sum)).astype(jnp.bfloat16)
    sum_high = row_sum.astype(jnp.bfloat16).astype(jnp.float32)
    sum_low = row_sum - sum_high
    lane = lax.broadcasted_iota(jnp.int32, (rows, HD), 1)
    row = lax.broadcasted_iota(jnp.int32, (rows, HD), 0)
    spread = jnp.where(lane == row, reference, 0.0)
    spread = jnp.where(lane == row + rows, sum_high, spread)
    spread = jnp.where(lane == row + 2 * rows, sum_low, spread)
    stats = jnp.sum(spread, axis=0, keepdims=True)
    tail = jnp.dot(place_key_ref[...], span_k, preferred_element_type=jnp.float32)
    tail = tail + jnp.dot(place_value_ref[...], span_v, preferred_element_type=jnp.float32)
    within = lax.broadcasted_iota(jnp.int32, tail.shape, 0) % TAIL
    tail = jnp.where(within == 2 * CAP, jnp.broadcast_to(stats, tail.shape), tail)
    out_ref[:, rows:, :] = tail.astype(jnp.bfloat16).reshape(seq_count, TAIL, HD)
    for dest in range(seq_count):
        out_ref[dest, :rows, :] = shared


def span_part(parts, cache_state, seq_count):
    rows = cache_state[0].shape[0]
    return pl.pallas_call(
        span_kernel,
        in_specs=[whole()] * (1 + len(cache_state)),
        out_specs=whole(),
        out_shape=jax.ShapeDtypeStruct((seq_count, rows + TAIL, HD), jnp.bfloat16),
        compiler_params=pltpu.CompilerParams(vmem_limit_bytes=8 * MIB),
        name="span_part",
    )(parts, *cache_state)


def out_kernel(requests, message_ref, weight_ref, out_ref):
    seq_count = message_ref.shape[0]
    rows = message_ref.shape[1] - TAIL
    per_group = rows // requests
    tails = message_ref[:, rows:, :].astype(jnp.float32)
    within = lax.broadcasted_iota(jnp.int32, tails.shape, 1)
    stats = jnp.sum(jnp.where(within == 2 * CAP, tails, 0.0), axis=1)
    m = stats[:, :rows]
    sums = stats[:, rows : 2 * rows] + stats[:, 2 * rows : 3 * rows]
    share = jnp.exp(m - jnp.max(m, axis=0, keepdims=True)) * sums
    share = share / jnp.sum(share, axis=0, keepdims=True)
    share = share.T
    total = jnp.zeros((rows, HD), jnp.float32)
    for source in range(seq_count):
        total = total + share[:, source : source + 1] * message_ref[source, :rows, :].astype(
            jnp.float32
        )
    attended = jnp.concatenate(
        [total[h * requests : (h + 1) * requests] for h in range(per_group)], axis=1
    ).astype(jnp.bfloat16)
    projected = jnp.dot(attended, weight_ref[...], preferred_element_type=jnp.float32)
    for dest in range(out_ref.shape[0]):
        out_ref[dest] = projected


def out_part(messages, out_weight, requests, tp_count):
    return pl.pallas_call(
        functools.partial(out_kernel, requests),
        in_specs=[whole()] * 2,
        out_specs=whole(),
        out_shape=jax.ShapeDtypeStruct((tp_count, requests, out_weight.shape[1]), jnp.float32),
        compiler_params=pltpu.CompilerParams(vmem_limit_bytes=8 * MIB),
        name="out_part",
    )(messages, out_weight)


def finish_kernel(
    message_ref, share_ref, out_hbm, key_hbm, value_hbm, out_ref, key_ref, value_ref, sems
):
    rows = message_ref.shape[1] - TAIL
    tails = message_ref[:, rows:, :]
    count = tails.shape[0]
    tails = jnp.concatenate(
        [tails[p : p + 1] for p in (listed(seq) for seq in range(count))], axis=0
    )
    key_ref[...] = tails[:, :CAP].reshape(key_ref.shape)
    value_ref[...] = tails[:, CAP : 2 * CAP].reshape(value_ref.shape)
    copies = [
        pltpu.make_async_copy(source, dest, sems.at[i])
        for i, (source, dest) in enumerate(
            ((out_ref, out_hbm), (key_ref, key_hbm), (value_ref, value_hbm))
        )
    ]
    copies[1].start()
    copies[2].start()
    out_ref[...] = jnp.sum(share_ref[...], axis=0).astype(jnp.bfloat16)
    copies[0].start()
    for copy in copies:
        copy.wait()


def finish(messages, shares):
    slots = jax.ShapeDtypeStruct((messages.shape[0] * CAP, HD), jnp.bfloat16)
    outs = [jax.ShapeDtypeStruct(shares.shape[1:], jnp.bfloat16), slots, slots]
    return pl.pallas_call(
        finish_kernel,
        in_specs=[whole()] * 2,
        out_specs=[whole(pltpu.HBM)] * 3,
        out_shape=outs,
        scratch_shapes=[VMEM(a.shape, a.dtype) for a in outs] + [pltpu.SemaphoreType.DMA((3,))],
        compiler_params=pltpu.CompilerParams(vmem_limit_bytes=8 * MIB),
        name="finish",
    )(messages, shares)


def per_device(
    decode_query,
    cache_keys,
    cache_values,
    cache_len,
    prefill_rows,
    key_weight,
    value_weight,
    span_request,
    span_target,
    out_weight,
):
    seq_count = lax.axis_size("seq")
    tp_count = lax.axis_size("tp")
    requests = cache_keys.shape[0]
    rows = requests * decode_query.shape[1] // HD
    pre_dev = prefill_rows.shape[0] // seq_count

    own, *sent = project(prefill_rows, key_weight, value_weight)
    seq = [(y, z) for y in range(NY) for z in range(NZ)]
    came = [
        lax.ppermute(part, "seq", [(y * NZ + z, (y + k) % NY * NZ + z) for y, z in seq])
        for k, part in zip(Y_STEPS, sent)
    ]
    targets = span_target.T
    request_ids = span_request.reshape(targets.shape)
    cache_state = cache_part(
        cache_len, decode_query, cache_keys, cache_values, targets, request_ids, seq_count
    )
    partial = fold(cache_state[0], [own, *came]).reshape(NZ, pre_dev, 2 * HD)
    parts = lax.all_to_all(
        partial,
        "seq",
        split_axis=0,
        concat_axis=0,
        tiled=True,
        axis_index_groups=[[y * NZ + z for z in reversed(range(NZ))] for y in range(NY)],
    )
    outgoing = span_part(parts, cache_state, seq_count)
    messages = lax.all_to_all(
        outgoing,
        "seq",
        split_axis=0,
        concat_axis=0,
        tiled=True,
        axis_index_groups=[[listed(place) for place in range(seq_count)]],
    )
    shares = out_part(messages, out_weight, requests, tp_count)
    shares = lax.all_to_all(
        shares,
        "tp",
        split_axis=0,
        concat_axis=0,
        tiled=True,
        axis_index_groups=[list(reversed(range(tp_count)))],
    )
    return finish(messages, shares)


def solution(mesh):
    placed = (
        P(None, "tp"),
        P(None, "seq", "tp"),
        P(None, "seq", "tp"),
        P(),
        P(None, "seq"),
        P("seq", "tp"),
        P("seq", "tp"),
        P(),
        P(),
        P("tp", "seq"),
    )
    return jax.shard_map(
        per_device,
        mesh=mesh,
        in_specs=placed,
        out_specs=(P(None, "seq"), P("seq", "tp"), P("seq", "tp")),
        check_vma=False,
    )
```

```python
import functools

import jax
import jax.numpy as jnp
from jax import lax
from jax.experimental import pallas as pl
from jax.experimental.pallas import tpu as pltpu
from jax.sharding import PartitionSpec as P

H = 64
KVH = 8
HD = 128
CAP = 2
DEAD = -(2.0**100)
NY = 4
NZ = 8
Y_STEPS = (1, 3, 2)
TAIL = 8
VMEM = pltpu.VMEM
SMEM = pltpu.SMEM
MIB = 1 << 20


def listed(place):
    y = (place >> 3 & 1) * 2 + (place >> 4 & 1)
    z = (place & 1) * 4 + (place >> 1 & 1) * 2 + (place >> 2 & 1)
    return NY * NZ - 1 - (y * NZ + z)


def whole(space=VMEM):
    return pl.BlockSpec(memory_space=space)


def in_hbm(array):
    return pltpu.with_memory_space_constraint(array, pltpu.HBM)


def project_kernel(
    rows_hbm, key_hbm, value_hbm, own_ref, to1_ref, to2_ref, to3_ref, rows_ref, weight_ref, sems
):
    copies = [
        pltpu.make_async_copy(key_hbm, weight_ref.at[:, :HD], sems.at[0]),
        pltpu.make_async_copy(value_hbm, weight_ref.at[:, HD:], sems.at[1]),
        pltpu.make_async_copy(rows_hbm, rows_ref, sems.at[2]),
    ]
    for copy in copies:
        copy.start()
    for copy in copies:
        copy.wait()
    weight = weight_ref[...]
    y = lax.axis_index("seq") // NZ
    size = own_ref.shape[0]
    for k, ref in zip((0,) + Y_STEPS, (own_ref, to1_ref, to2_ref, to3_ref)):
        first = pl.multiple_of(lax.rem(y + k, NY) * size, size)
        ref[...] = jnp.dot(
            rows_ref[pl.ds(first, size), :], weight, preferred_element_type=jnp.float32
        ).astype(jnp.bfloat16)


def project(rows, key_weight, value_weight):
    tokens, features = rows.shape
    return pl.pallas_call(
        project_kernel,
        in_specs=[whole(pltpu.HBM)] * 3,
        out_specs=[whole()] * NY,
        out_shape=[jax.ShapeDtypeStruct((tokens // NY, 2 * HD), jnp.bfloat16)] * NY,
        scratch_shapes=[
            VMEM((tokens, features), jnp.bfloat16),
            VMEM((features, 2 * HD), jnp.bfloat16),
            pltpu.SemaphoreType.DMA((3,)),
        ],
        compiler_params=pltpu.CompilerParams(vmem_limit_bytes=8 * MIB),
        name="project",
    )(in_hbm(rows), in_hbm(key_weight), in_hbm(value_weight))


def fold_kernel(after_ref, own_ref, from1_ref, from2_ref, from3_ref, out_ref):
    total = own_ref[...].astype(jnp.float32)
    for ref in (from1_ref, from2_ref, from3_ref):
        total = total + ref[...].astype(jnp.float32)
    total = total.astype(jnp.bfloat16)
    size = total.shape[0] // NZ
    for z in range(NZ):
        place = listed(NY * NZ - NZ + z) * size
        out_ref[place : place + size, :] = total[z * size : (z + 1) * size]


def fold(after, parts):
    return pl.pallas_call(
        fold_kernel,
        in_specs=[whole()] * 5,
        out_specs=whole(),
        out_shape=jax.ShapeDtypeStruct(parts[0].shape, jnp.bfloat16),
        compiler_params=pltpu.CompilerParams(vmem_limit_bytes=8 * MIB),
        name="fold",
    )(after, *parts)


def stacked_queries(query_ref, per_group):
    query = query_ref[...]
    return jnp.concatenate(
        [query[:, h * HD : (h + 1) * HD] for h in range(per_group)], axis=0
    )


def cache_kernel(
    requests,
    per_group,
    len_hbm,
    query_hbm,
    target_hbm,
    request_hbm,
    keys_hbm,
    values_hbm,
    o_ref,
    m_ref,
    l_ref,
    place_key_ref,
    place_value_ref,
    live_ref,
    stacked_ref,
    len_ref,
    query_ref,
    target_ref,
    request_ref,
    keys_ref,
    values_ref,
    query_rows,
    o_rows,
    m_rows,
    l_rows,
    small_sems,
    sems,
):
    seq_index = lax.axis_index("seq")
    rows = requests * per_group
    local_len = keys_ref.shape[1]
    tokens = live_ref.shape[1]
    small = [
        pltpu.make_async_copy(source, dest, small_sems.at[i])
        for i, (source, dest) in enumerate(
            (
                (len_hbm, len_ref),
                (query_hbm, query_ref),
                (target_hbm, target_ref),
                (request_hbm, request_ref),
            )
        )
    ]
    key_copies = [
        pltpu.make_async_copy(keys_hbm.at[r], keys_ref.at[r], sems.at[0, r])
        for r in range(requests)
    ]
    value_copies = [
        pltpu.make_async_copy(values_hbm.at[r], values_ref.at[r], sems.at[1, r])
        for r in range(requests)
    ]
    for copy in small:
        copy.start()
    for r in range(requests):
        key_copies[r].start()
        value_copies[r].start()
    for copy in small:
        copy.wait()

    per_tile = HD // tokens
    first = pl.multiple_of(seq_index // per_tile * HD, HD)
    shift = lax.rem(HD - lax.rem(seq_index, per_tile) * tokens, HD)

    def own(ref):
        tile = jnp.broadcast_to(ref[:, pl.ds(first, HD)], (8, HD))
        return pltpu.roll(tile, shift, 1)[0:1, :tokens]

    target_row = own(target_ref)
    target = jnp.broadcast_to(target_row, (tokens, tokens))
    i = lax.broadcasted_iota(jnp.int32, (tokens, tokens), 0)
    j = lax.broadcasted_iota(jnp.int32, (tokens, tokens), 1)
    column = jnp.sum(jnp.where(i == j, target, 0), axis=1, keepdims=True)
    rank = jnp.sum(jnp.where((column == target) & (i < j), 1, 0), axis=0, keepdims=True)
    slot = target_row * CAP + rank
    count = place_key_ref.shape[0]
    row = lax.broadcasted_iota(jnp.int32, (count, tokens), 0)
    dest, within = listed(row // TAIL), row % TAIL
    wanted = jnp.broadcast_to(slot, (count, tokens))
    is_key = (within < CAP) & (wanted == dest * CAP + within)
    is_value = (within >= CAP) & (within < 2 * CAP) & (wanted == dest * CAP + within - CAP)
    place_key_ref[...] = jnp.where(is_key, 1.0, 0.0).astype(jnp.bfloat16)
    place_value_ref[...] = jnp.where(is_value, 1.0, 0.0).astype(jnp.bfloat16)
    owner = jnp.broadcast_to(own(request_ref), (rows, tokens))
    mine = lax.broadcasted_iota(jnp.int32, (rows, tokens), 0) % requests
    live_ref[...] = jnp.where(owner == mine, 1.0, 0.0)

    stacked = stacked_queries(query_ref, per_group)
    stacked_ref[...] = stacked
    query_rows[...] = stacked.astype(jnp.float32)
    for r in range(requests):
        query = query_rows[pl.ds(r, per_group, stride=requests), :].astype(jnp.bfloat16)
        key_copies[r].wait()
        scores = lax.dot_general(
            query, keys_ref[r], (((1,), (1,)), ((), ())), preferred_element_type=jnp.float32
        ) * HD ** (-0.5)
        position = seq_index * local_len + lax.broadcasted_iota(jnp.int32, scores.shape, 1)
        allowed = position < len_ref[r]
        scores = jnp.where(allowed, scores, DEAD)
        top = jnp.max(scores, axis=1, keepdims=True)
        weights = jnp.where(allowed, jnp.exp(scores - top), 0.0)
        own_rows = pl.ds(r * per_group, per_group)
        l_rows[own_rows, :] = jnp.broadcast_to(
            jnp.sum(weights, axis=1, keepdims=True), (per_group, HD)
        )
        m_rows[own_rows, :] = jnp.broadcast_to(top, (per_group, HD))
        value_copies[r].wait()
        o_rows[own_rows, :] = jnp.dot(
            weights.astype(jnp.bfloat16), values_ref[r], preferred_element_type=jnp.float32
        )
    for h in range(per_group):
        to = pl.ds(h * requests, requests)
        of = pl.ds(h, requests, stride=per_group)
        o_ref[to, :] = o_rows[of, :]
        m_ref[to, :] = m_rows[of, :]
        l_ref[to, :] = l_rows[of, :]


def cache_part(cache_len, query, keys, values, target, request_ids, seq_count):
    requests, local_len, _ = keys.shape
    per_group = query.shape[1] // HD
    rows = requests * per_group
    tokens = target.shape[1] // seq_count
    f32 = jnp.float32
    table = jax.ShapeDtypeStruct((rows, HD), f32)
    place = jax.ShapeDtypeStruct((seq_count * TAIL, tokens), jnp.bfloat16)
    operands = (cache_len, query, target, request_ids, keys, values)
    return pl.pallas_call(
        functools.partial(cache_kernel, requests, per_group),
        in_specs=[whole(pltpu.HBM)] * 6,
        out_specs=[whole()] * 7,
        out_shape=[
            table,
            table,
            table,
            place,
            place,
            jax.ShapeDtypeStruct((rows, tokens), f32),
            jax.ShapeDtypeStruct((rows, HD), query.dtype),
        ],
        scratch_shapes=[SMEM(cache_len.shape, cache_len.dtype)]
        + [VMEM(a.shape, a.dtype) for a in operands[1:]]
        + [VMEM((rows, HD), f32)] * 4
        + [pltpu.SemaphoreType.DMA((4,)), pltpu.SemaphoreType.DMA((2, requests))],
        cost_estimate=pl.CostEstimate(
            flops=4 * rows * local_len * HD,
            bytes_accessed=4 * requests * local_len * HD,
            transcendentals=rows * local_len,
        ),
        compiler_params=pltpu.CompilerParams(vmem_limit_bytes=16 * MIB),
        name="cache_part",
    )(*[in_hbm(a) for a in operands])


def span_kernel(
    parts_ref,
    o_ref,
    m_ref,
    l_ref,
    place_key_ref,
    place_value_ref,
    live_ref,
    query_ref,
    out_ref,
):
    rows = o_ref.shape[0]
    seq_count = out_ref.shape[0]
    total = parts_ref[0].astype(jnp.float32)
    for source in range(1, parts_ref.shape[0]):
        total = total + parts_ref[source].astype(jnp.float32)
    owned = total.astype(jnp.bfloat16)
    span_k, span_v = owned[:, :HD], owned[:, HD:]
    live = live_ref[...] > 0.5
    scores = lax.dot_general(
        query_ref[...], span_k, (((1,), (1,)), ((), ())), preferred_element_type=jnp.float32
    ) * HD ** (-0.5)
    scores = jnp.where(live, scores, DEAD)
    m_cache = m_ref[:, 0:1]
    reference = (
        jnp.maximum(m_cache, jnp.max(scores, axis=1, keepdims=True))
        .astype(jnp.bfloat16)
        .astype(jnp.float32)
    )
    weights = jnp.where(live, jnp.exp(scores - reference), 0.0)
    scale = jnp.exp(m_cache - reference)
    row_sum = scale * l_ref[:, 0:1] + jnp.sum(weights, axis=1, keepdims=True)
    weighted = scale * o_ref[...] + jnp.dot(
        weights.astype(jnp.bfloat16), span_v, preferred_element_type=jnp.float32
    )
    empty = row_sum == 0.0
    shared = jnp.where(empty, 0.0, weighted / jnp.where(empty, 1.0, row_sum)).astype(jnp.bfloat16)
    sum_high = row_sum.astype(jnp.bfloat16).astype(jnp.float32)
    sum_low = row_sum - sum_high
    lane = lax.broadcasted_iota(jnp.int32, (rows, HD), 1)
    row = lax.broadcasted_iota(jnp.int32, (rows, HD), 0)
    spread = jnp.where(lane == row, reference, 0.0)
    spread = jnp.where(lane == row + rows, sum_high, spread)
    spread = jnp.where(lane == row + 2 * rows, sum_low, spread)
    stats = jnp.sum(spread, axis=0, keepdims=True)
    tail = jnp.dot(place_key_ref[...], span_k, preferred_element_type=jnp.float32)
    tail = tail + jnp.dot(place_value_ref[...], span_v, preferred_element_type=jnp.float32)
    within = lax.broadcasted_iota(jnp.int32, tail.shape, 0) % TAIL
    tail = jnp.where(within == 2 * CAP, jnp.broadcast_to(stats, tail.shape), tail)
    out_ref[:, rows:, :] = tail.astype(jnp.bfloat16).reshape(seq_count, TAIL, HD)
    for dest in range(seq_count):
        out_ref[dest, :rows, :] = shared


def span_part(parts, cache_state, seq_count):
    rows = cache_state[0].shape[0]
    return pl.pallas_call(
        span_kernel,
        in_specs=[whole()] * (1 + len(cache_state)),
        out_specs=whole(),
        out_shape=jax.ShapeDtypeStruct((seq_count, rows + TAIL, HD), jnp.bfloat16),
        compiler_params=pltpu.CompilerParams(vmem_limit_bytes=8 * MIB),
        name="span_part",
    )(parts, *cache_state)


def out_kernel(requests, message_ref, weight_ref, out_ref):
    seq_count = message_ref.shape[0]
    rows = message_ref.shape[1] - TAIL
    per_group = rows // requests
    tails = message_ref[:, rows:, :].astype(jnp.float32)
    within = lax.broadcasted_iota(jnp.int32, tails.shape, 1)
    stats = jnp.sum(jnp.where(within == 2 * CAP, tails, 0.0), axis=1)
    m = stats[:, :rows]
    sums = stats[:, rows : 2 * rows] + stats[:, 2 * rows : 3 * rows]
    share = jnp.exp(m - jnp.max(m, axis=0, keepdims=True)) * sums
    share = share / jnp.sum(share, axis=0, keepdims=True)
    share = share.T
    total = jnp.zeros((rows, HD), jnp.float32)
    for source in range(seq_count):
        total = total + share[:, source : source + 1] * message_ref[source, :rows, :].astype(
            jnp.float32
        )
    attended = jnp.concatenate(
        [total[h * requests : (h + 1) * requests] for h in range(per_group)], axis=1
    ).astype(jnp.bfloat16)
    projected = jnp.dot(attended, weight_ref[...], preferred_element_type=jnp.float32)
    for dest in range(out_ref.shape[0]):
        out_ref[dest] = projected


def out_part(messages, out_weight, requests, tp_count):
    return pl.pallas_call(
        functools.partial(out_kernel, requests),
        in_specs=[whole()] * 2,
        out_specs=whole(),
        out_shape=jax.ShapeDtypeStruct((tp_count, requests, out_weight.shape[1]), jnp.float32),
        compiler_params=pltpu.CompilerParams(vmem_limit_bytes=8 * MIB),
        name="out_part",
    )(messages, out_weight)


def finish_kernel(
    message_ref, share_ref, out_hbm, key_hbm, value_hbm, out_ref, key_ref, value_ref, sems
):
    rows = message_ref.shape[1] - TAIL
    tails = message_ref[:, rows:, :]
    count = tails.shape[0]
    tails = jnp.concatenate(
        [tails[p : p + 1] for p in (listed(seq) for seq in range(count))], axis=0
    )
    key_ref[...] = tails[:, :CAP].reshape(key_ref.shape)
    value_ref[...] = tails[:, CAP : 2 * CAP].reshape(value_ref.shape)
    copies = [
        pltpu.make_async_copy(source, dest, sems.at[i])
        for i, (source, dest) in enumerate(
            ((out_ref, out_hbm), (key_ref, key_hbm), (value_ref, value_hbm))
        )
    ]
    copies[1].start()
    copies[2].start()
    out_ref[...] = jnp.sum(share_ref[...], axis=0).astype(jnp.bfloat16)
    copies[0].start()
    for copy in copies:
        copy.wait()


def finish(messages, shares):
    slots = jax.ShapeDtypeStruct((messages.shape[0] * CAP, HD), jnp.bfloat16)
    outs = [jax.ShapeDtypeStruct(shares.shape[1:], jnp.bfloat16), slots, slots]
    return pl.pallas_call(
        finish_kernel,
        in_specs=[whole()] * 2,
        out_specs=[whole(pltpu.HBM)] * 3,
        out_shape=outs,
        scratch_shapes=[VMEM(a.shape, a.dtype) for a in outs] + [pltpu.SemaphoreType.DMA((3,))],
        compiler_params=pltpu.CompilerParams(vmem_limit_bytes=8 * MIB),
        name="finish",
    )(messages, shares)


def per_device(
    decode_query,
    cache_keys,
    cache_values,
    cache_len,
    prefill_rows,
    key_weight,
    value_weight,
    span_request,
    span_target,
    out_weight,
):
    seq_count = lax.axis_size("seq")
    tp_count = lax.axis_size("tp")
    requests = cache_keys.shape[0]
    rows = requests * decode_query.shape[1] // HD
    pre_dev = prefill_rows.shape[0] // seq_count

    own, *sent = project(prefill_rows, key_weight, value_weight)
    seq = [(y, z) for y in range(NY) for z in range(NZ)]
    came = [
        lax.ppermute(part, "seq", [(y * NZ + z, (y + k) % NY * NZ + z) for y, z in seq])
        for k, part in zip(Y_STEPS, sent)
    ]
    targets = span_target.T
    request_ids = span_request.reshape(targets.shape)
    cache_state = cache_part(
        cache_len, decode_query, cache_keys, cache_values, targets, request_ids, seq_count
    )
    z_order = [listed(NY * NZ - NZ + place) for place in range(NZ)]
    partial = fold(cache_state[0], [own, *came]).reshape(NZ, pre_dev, 2 * HD)
    parts = lax.all_to_all(
        partial,
        "seq",
        split_axis=0,
        concat_axis=0,
        tiled=True,
        axis_index_groups=[[y * NZ + z for z in z_order] for y in range(NY)],
    )
    outgoing = span_part(parts, cache_state, seq_count)
    messages = lax.all_to_all(
        outgoing,
        "seq",
        split_axis=0,
        concat_axis=0,
        tiled=True,
        axis_index_groups=[[listed(place) for place in range(seq_count)]],
    )
    shares = out_part(messages, out_weight, requests, tp_count)
    shares = lax.all_to_all(
        shares,
        "tp",
        split_axis=0,
        concat_axis=0,
        tiled=True,
        axis_index_groups=[list(reversed(range(tp_count)))],
    )
    return finish(messages, shares)


def solution(mesh):
    placed = (
        P(None, "tp"),
        P(None, "seq", "tp"),
        P(None, "seq", "tp"),
        P(),
        P(None, "seq"),
        P("seq", "tp"),
        P("seq", "tp"),
        P(),
        P(),
        P("tp", "seq"),
    )
    return jax.shard_map(
        per_device,
        mesh=mesh,
        in_specs=placed,
        out_specs=(P(None, "seq"), P("seq", "tp"), P("seq", "tp")),
        check_vma=False,
    )
```

```python
import functools

import jax
import jax.numpy as jnp
from jax import lax
from jax.experimental import pallas as pl
from jax.experimental.pallas import tpu as pltpu
from jax.sharding import PartitionSpec as P

H = 64
KVH = 8
HD = 128
CAP = 2
DEAD = -(2.0**100)
NY = 4
NZ = 8
Y_STEPS = (1, 3, 2)
TAIL = 8
VMEM = pltpu.VMEM
SMEM = pltpu.SMEM
MIB = 1 << 20


def listed(place):
    y = (place >> 3 & 1) * 2 + (place >> 4 & 1)
    z = (place & 1) * 4 + (place >> 1 & 1) * 2 + (place >> 2 & 1)
    return NY * NZ - 1 - (y * NZ + z)


def whole(space=VMEM):
    return pl.BlockSpec(memory_space=space)


def in_hbm(array):
    return pltpu.with_memory_space_constraint(array, pltpu.HBM)


def project_kernel(
    rows_hbm, key_hbm, value_hbm, own_ref, to1_ref, to2_ref, to3_ref, rows_ref, weight_ref, sems
):
    copies = [
        pltpu.make_async_copy(key_hbm, weight_ref.at[:, :HD], sems.at[0]),
        pltpu.make_async_copy(value_hbm, weight_ref.at[:, HD:], sems.at[1]),
        pltpu.make_async_copy(rows_hbm, rows_ref, sems.at[2]),
    ]
    for copy in copies:
        copy.start()
    for copy in copies:
        copy.wait()
    weight = weight_ref[...]
    y = lax.axis_index("seq") // NZ
    size = own_ref.shape[0]
    for k, ref in zip((0,) + Y_STEPS, (own_ref, to1_ref, to2_ref, to3_ref)):
        first = pl.multiple_of((y ^ k) * size, size)
        ref[...] = jnp.dot(
            rows_ref[pl.ds(first, size), :], weight, preferred_element_type=jnp.float32
        ).astype(ref.dtype)


def project(rows, key_weight, value_weight):
    tokens, features = rows.shape
    return pl.pallas_call(
        project_kernel,
        in_specs=[whole(pltpu.HBM)] * 3,
        out_specs=[whole()] * NY,
        out_shape=[jax.ShapeDtypeStruct((tokens // NY, 2 * HD), jnp.float32)]
        + [jax.ShapeDtypeStruct((tokens // NY, 2 * HD), jnp.bfloat16)] * (NY - 1),
        scratch_shapes=[
            VMEM((tokens, features), jnp.bfloat16),
            VMEM((features, 2 * HD), jnp.bfloat16),
            pltpu.SemaphoreType.DMA((3,)),
        ],
        compiler_params=pltpu.CompilerParams(vmem_limit_bytes=8 * MIB),
        name="project",
    )(in_hbm(rows), in_hbm(key_weight), in_hbm(value_weight))


def fold_kernel(after_ref, own_ref, from1_ref, from2_ref, from3_ref, out_ref):
    total = own_ref[...]
    for ref in (from1_ref, from2_ref, from3_ref):
        total = total + ref[...].astype(jnp.float32)
    total = total.astype(jnp.bfloat16)
    size = total.shape[0] // NZ
    for z in range(NZ):
        place = listed(NY * NZ - NZ + z) * size
        out_ref[place : place + size, :] = total[z * size : (z + 1) * size]


def fold(after, parts):
    return pl.pallas_call(
        fold_kernel,
        in_specs=[whole()] * 5,
        out_specs=whole(),
        out_shape=jax.ShapeDtypeStruct(parts[0].shape, parts[1].dtype),
        compiler_params=pltpu.CompilerParams(vmem_limit_bytes=8 * MIB),
        name="fold",
    )(after, *parts)


def stacked_queries(query_ref, per_group):
    query = query_ref[...]
    return jnp.concatenate(
        [query[:, h * HD : (h + 1) * HD] for h in range(per_group)], axis=0
    )


def cache_kernel(
    requests,
    per_group,
    len_hbm,
    query_hbm,
    target_hbm,
    request_hbm,
    keys_hbm,
    values_hbm,
    o_ref,
    m_ref,
    l_ref,
    place_key_ref,
    place_value_ref,
    live_ref,
    stacked_ref,
    len_ref,
    query_ref,
    target_ref,
    request_ref,
    keys_ref,
    values_ref,
    query_rows,
    o_rows,
    m_rows,
    l_rows,
    small_sems,
    sems,
):
    seq_index = lax.axis_index("seq")
    rows = requests * per_group
    local_len = keys_ref.shape[1]
    tokens = live_ref.shape[1]
    small = [
        pltpu.make_async_copy(source, dest, small_sems.at[i])
        for i, (source, dest) in enumerate(
            (
                (len_hbm, len_ref),
                (query_hbm, query_ref),
                (target_hbm, target_ref),
                (request_hbm, request_ref),
            )
        )
    ]
    key_copies = [
        pltpu.make_async_copy(keys_hbm.at[r], keys_ref.at[r], sems.at[0, r])
        for r in range(requests)
    ]
    value_copies = [
        pltpu.make_async_copy(values_hbm.at[r], values_ref.at[r], sems.at[1, r])
        for r in range(requests)
    ]
    for copy in small:
        copy.start()
    for r in range(requests):
        key_copies[r].start()
        value_copies[r].start()
    for copy in small:
        copy.wait()

    per_tile = HD // tokens
    first = pl.multiple_of(seq_index // per_tile * HD, HD)
    shift = lax.rem(HD - lax.rem(seq_index, per_tile) * tokens, HD)

    def own(ref):
        tile = jnp.broadcast_to(ref[:, pl.ds(first, HD)], (8, HD))
        return pltpu.roll(tile, shift, 1)[0:1, :tokens]

    target_row = own(target_ref)
    target = jnp.broadcast_to(target_row, (tokens, tokens))
    i = lax.broadcasted_iota(jnp.int32, (tokens, tokens), 0)
    j = lax.broadcasted_iota(jnp.int32, (tokens, tokens), 1)
    column = jnp.sum(jnp.where(i == j, target, 0), axis=1, keepdims=True)
    rank = jnp.sum(jnp.where((column == target) & (i < j), 1, 0), axis=0, keepdims=True)
    slot = target_row * CAP + rank
    count = place_key_ref.shape[0]
    row = lax.broadcasted_iota(jnp.int32, (count, tokens), 0)
    dest, within = listed(row // TAIL), row % TAIL
    wanted = jnp.broadcast_to(slot, (count, tokens))
    is_key = (within < CAP) & (wanted == dest * CAP + within)
    is_value = (within >= CAP) & (within < 2 * CAP) & (wanted == dest * CAP + within - CAP)
    place_key_ref[...] = jnp.where(is_key, 1.0, 0.0).astype(jnp.bfloat16)
    place_value_ref[...] = jnp.where(is_value, 1.0, 0.0).astype(jnp.bfloat16)
    owner = jnp.broadcast_to(own(request_ref), (rows, tokens))
    mine = lax.broadcasted_iota(jnp.int32, (rows, tokens), 0) % requests
    live_ref[...] = jnp.where(owner == mine, 1.0, 0.0)

    stacked = stacked_queries(query_ref, per_group)
    stacked_ref[...] = stacked
    query_rows[...] = stacked.astype(jnp.float32)
    for r in range(requests):
        query = query_rows[pl.ds(r, per_group, stride=requests), :].astype(jnp.bfloat16)
        key_copies[r].wait()
        scores = lax.dot_general(
            query, keys_ref[r], (((1,), (1,)), ((), ())), preferred_element_type=jnp.float32
        ) * HD ** (-0.5)
        position = seq_index * local_len + lax.broadcasted_iota(jnp.int32, scores.shape, 1)
        allowed = position < len_ref[r]
        scores = jnp.where(allowed, scores, DEAD)
        top = jnp.max(scores, axis=1, keepdims=True)
        weights = jnp.where(allowed, jnp.exp(scores - top), 0.0)
        own_rows = pl.ds(r * per_group, per_group)
        l_rows[own_rows, :] = jnp.broadcast_to(
            jnp.sum(weights, axis=1, keepdims=True), (per_group, HD)
        )
        m_rows[own_rows, :] = jnp.broadcast_to(top, (per_group, HD))
        value_copies[r].wait()
        o_rows[own_rows, :] = jnp.dot(
            weights.astype(jnp.bfloat16), values_ref[r], preferred_element_type=jnp.float32
        )
    for h in range(per_group):
        to = pl.ds(h * requests, requests)
        of = pl.ds(h, requests, stride=per_group)
        o_ref[to, :] = o_rows[of, :]
        m_ref[to, :] = m_rows[of, :]
        l_ref[to, :] = l_rows[of, :]


def cache_part(cache_len, query, keys, values, target, request_ids, seq_count):
    requests, local_len, _ = keys.shape
    per_group = query.shape[1] // HD
    rows = requests * per_group
    tokens = target.shape[1] // seq_count
    f32 = jnp.float32
    table = jax.ShapeDtypeStruct((rows, HD), f32)
    place = jax.ShapeDtypeStruct((seq_count * TAIL, tokens), jnp.bfloat16)
    operands = (cache_len, query, target, request_ids, keys, values)
    return pl.pallas_call(
        functools.partial(cache_kernel, requests, per_group),
        in_specs=[whole(pltpu.HBM)] * 6,
        out_specs=[whole()] * 7,
        out_shape=[
            table,
            table,
            table,
            place,
            place,
            jax.ShapeDtypeStruct((rows, tokens), f32),
            jax.ShapeDtypeStruct((rows, HD), query.dtype),
        ],
        scratch_shapes=[SMEM(cache_len.shape, cache_len.dtype)]
        + [VMEM(a.shape, a.dtype) for a in operands[1:]]
        + [VMEM((rows, HD), f32)] * 4
        + [pltpu.SemaphoreType.DMA((4,)), pltpu.SemaphoreType.DMA((2, requests))],
        cost_estimate=pl.CostEstimate(
            flops=4 * rows * local_len * HD,
            bytes_accessed=4 * requests * local_len * HD,
            transcendentals=rows * local_len,
        ),
        compiler_params=pltpu.CompilerParams(vmem_limit_bytes=16 * MIB),
        name="cache_part",
    )(*[in_hbm(a) for a in operands])


def span_kernel(
    parts_ref,
    o_ref,
    m_ref,
    l_ref,
    place_key_ref,
    place_value_ref,
    live_ref,
    query_ref,
    out_ref,
):
    rows = o_ref.shape[0]
    seq_count = out_ref.shape[0]
    total = parts_ref[0].astype(jnp.float32)
    for source in range(1, parts_ref.shape[0]):
        total = total + parts_ref[source].astype(jnp.float32)
    owned = total.astype(jnp.bfloat16)
    span_k, span_v = owned[:, :HD], owned[:, HD:]
    live = live_ref[...] > 0.5
    scores = lax.dot_general(
        query_ref[...], span_k, (((1,), (1,)), ((), ())), preferred_element_type=jnp.float32
    ) * HD ** (-0.5)
    scores = jnp.where(live, scores, DEAD)
    m_cache = m_ref[:, 0:1]
    reference = (
        jnp.maximum(m_cache, jnp.max(scores, axis=1, keepdims=True))
        .astype(jnp.bfloat16)
        .astype(jnp.float32)
    )
    weights = jnp.where(live, jnp.exp(scores - reference), 0.0)
    scale = jnp.exp(m_cache - reference)
    row_sum = scale * l_ref[:, 0:1] + jnp.sum(weights, axis=1, keepdims=True)
    weighted = scale * o_ref[...] + jnp.dot(
        weights.astype(jnp.bfloat16), span_v, preferred_element_type=jnp.float32
    )
    empty = row_sum == 0.0
    shared = jnp.where(empty, 0.0, weighted / jnp.where(empty, 1.0, row_sum)).astype(jnp.bfloat16)
    sum_high = row_sum.astype(jnp.bfloat16).astype(jnp.float32)
    sum_low = row_sum - sum_high
    lane = lax.broadcasted_iota(jnp.int32, (rows, HD), 1)
    row = lax.broadcasted_iota(jnp.int32, (rows, HD), 0)
    spread = jnp.where(lane == row, reference, 0.0)
    spread = jnp.where(lane == row + rows, sum_high, spread)
    spread = jnp.where(lane == row + 2 * rows, sum_low, spread)
    stats = jnp.sum(spread, axis=0, keepdims=True)
    tail = jnp.dot(place_key_ref[...], span_k, preferred_element_type=jnp.float32)
    tail = tail + jnp.dot(place_value_ref[...], span_v, preferred_element_type=jnp.float32)
    within = lax.broadcasted_iota(jnp.int32, tail.shape, 0) % TAIL
    tail = jnp.where(within == 2 * CAP, jnp.broadcast_to(stats, tail.shape), tail)
    out_ref[:, rows:, :] = tail.astype(jnp.bfloat16).reshape(seq_count, TAIL, HD)
    for dest in range(seq_count):
        out_ref[dest, :rows, :] = shared


def span_part(parts, cache_state, seq_count):
    rows = cache_state[0].shape[0]
    return pl.pallas_call(
        span_kernel,
        in_specs=[whole()] * (1 + len(cache_state)),
        out_specs=whole(),
        out_shape=jax.ShapeDtypeStruct((seq_count, rows + TAIL, HD), jnp.bfloat16),
        compiler_params=pltpu.CompilerParams(vmem_limit_bytes=8 * MIB),
        name="span_part",
    )(parts, *cache_state)


def out_kernel(requests, message_ref, weight_ref, out_ref):
    seq_count = message_ref.shape[0]
    rows = message_ref.shape[1] - TAIL
    per_group = rows // requests
    tails = message_ref[:, rows:, :].astype(jnp.float32)
    within = lax.broadcasted_iota(jnp.int32, tails.shape, 1)
    stats = jnp.sum(jnp.where(within == 2 * CAP, tails, 0.0), axis=1)
    m = stats[:, :rows]
    sums = stats[:, rows : 2 * rows] + stats[:, 2 * rows : 3 * rows]
    share = jnp.exp(m - jnp.max(m, axis=0, keepdims=True)) * sums
    share = share / jnp.sum(share, axis=0, keepdims=True)
    share = share.T
    total = jnp.zeros((rows, HD), jnp.float32)
    for source in range(seq_count):
        total = total + share[:, source : source + 1] * message_ref[source, :rows, :].astype(
            jnp.float32
        )
    attended = jnp.concatenate(
        [total[h * requests : (h + 1) * requests] for h in range(per_group)], axis=1
    ).astype(jnp.bfloat16)
    projected = jnp.dot(attended, weight_ref[...], preferred_element_type=jnp.float32)
    for dest in range(out_ref.shape[0]):
        out_ref[dest] = projected


def out_part(messages, out_weight, requests, tp_count):
    return pl.pallas_call(
        functools.partial(out_kernel, requests),
        in_specs=[whole()] * 2,
        out_specs=whole(),
        out_shape=jax.ShapeDtypeStruct((tp_count, requests, out_weight.shape[1]), jnp.float32),
        compiler_params=pltpu.CompilerParams(vmem_limit_bytes=8 * MIB),
        name="out_part",
    )(messages, out_weight)


def finish_kernel(
    message_ref, share_ref, out_hbm, key_hbm, value_hbm, out_ref, key_ref, value_ref, sems
):
    rows = message_ref.shape[1] - TAIL
    tails = message_ref[:, rows:, :]
    count = tails.shape[0]
    tails = jnp.concatenate(
        [tails[p : p + 1] for p in (listed(seq) for seq in range(count))], axis=0
    )
    key_ref[...] = tails[:, :CAP].reshape(key_ref.shape)
    value_ref[...] = tails[:, CAP : 2 * CAP].reshape(value_ref.shape)
    copies = [
        pltpu.make_async_copy(source, dest, sems.at[i])
        for i, (source, dest) in enumerate(
            ((out_ref, out_hbm), (key_ref, key_hbm), (value_ref, value_hbm))
        )
    ]
    copies[1].start()
    copies[2].start()
    out_ref[...] = jnp.sum(share_ref[...], axis=0).astype(jnp.bfloat16)
    copies[0].start()
    for copy in copies:
        copy.wait()


def finish(messages, shares):
    slots = jax.ShapeDtypeStruct((messages.shape[0] * CAP, HD), jnp.bfloat16)
    outs = [jax.ShapeDtypeStruct(shares.shape[1:], jnp.bfloat16), slots, slots]
    return pl.pallas_call(
        finish_kernel,
        in_specs=[whole()] * 2,
        out_specs=[whole(pltpu.HBM)] * 3,
        out_shape=outs,
        scratch_shapes=[VMEM(a.shape, a.dtype) for a in outs] + [pltpu.SemaphoreType.DMA((3,))],
        compiler_params=pltpu.CompilerParams(vmem_limit_bytes=8 * MIB),
        name="finish",
    )(messages, shares)


def per_device(
    decode_query,
    cache_keys,
    cache_values,
    cache_len,
    prefill_rows,
    key_weight,
    value_weight,
    span_request,
    span_target,
    out_weight,
):
    seq_count = lax.axis_size("seq")
    tp_count = lax.axis_size("tp")
    requests = cache_keys.shape[0]
    rows = requests * decode_query.shape[1] // HD
    pre_dev = prefill_rows.shape[0] // seq_count

    own, *sent = project(prefill_rows, key_weight, value_weight)
    seq = [(y, z) for y in range(NY) for z in range(NZ)]
    came = [
        lax.ppermute(part, "seq", [(y * NZ + z, (y ^ k) * NZ + z) for y, z in seq])
        for k, part in zip(Y_STEPS, sent)
    ]
    targets = span_target.T
    request_ids = span_request.reshape(targets.shape)
    cache_state = cache_part(
        cache_len, decode_query, cache_keys, cache_values, targets, request_ids, seq_count
    )
    z_order = [listed(NY * NZ - NZ + place) for place in range(NZ)]
    partial = fold(cache_state[0], [own, *came]).reshape(NZ, pre_dev, 2 * HD)
    parts = lax.all_to_all(
        partial,
        "seq",
        split_axis=0,
        concat_axis=0,
        tiled=True,
        axis_index_groups=[[y * NZ + z for z in z_order] for y in range(NY)],
    )
    outgoing = span_part(parts, cache_state, seq_count)
    messages = lax.all_to_all(
        outgoing,
        "seq",
        split_axis=0,
        concat_axis=0,
        tiled=True,
        axis_index_groups=[[listed(place) for place in range(seq_count)]],
    )
    shares = out_part(messages, out_weight, requests, tp_count)
    shares = lax.all_to_all(
        shares,
        "tp",
        split_axis=0,
        concat_axis=0,
        tiled=True,
        axis_index_groups=[list(reversed(range(tp_count)))],
    )
    return finish(messages, shares)


def solution(mesh):
    placed = (
        P(None, "tp"),
        P(None, "seq", "tp"),
        P(None, "seq", "tp"),
        P(),
        P(None, "seq"),
        P("seq", "tp"),
        P("seq", "tp"),
        P(),
        P(),
        P("tp", "seq"),
    )
    return jax.shard_map(
        per_device,
        mesh=mesh,
        in_specs=placed,
        out_specs=(P(None, "seq"), P("seq", "tp"), P("seq", "tp")),
        check_vma=False,
    )
```

```python
import functools

import jax
import jax.numpy as jnp
from jax import lax
from jax.experimental import pallas as pl
from jax.experimental.pallas import tpu as pltpu
from jax.sharding import PartitionSpec as P

H = 64
KVH = 8
HD = 128
CAP = 2
DEAD = -(2.0**100)
NY = 4
NZ = 8
Y_STEPS = (1, 3, 2)
TAIL = 8
VMEM = pltpu.VMEM
SMEM = pltpu.SMEM
MIB = 1 << 20


def listed(place):
    y = (place >> 3 & 1) * 2 + (place >> 4 & 1)
    z = (place & 1) * 4 + (place >> 1 & 1) * 2 + (place >> 2 & 1)
    return NY * NZ - 1 - (y * NZ + z)


def whole(space=VMEM):
    return pl.BlockSpec(memory_space=space)


def in_hbm(array):
    return pltpu.with_memory_space_constraint(array, pltpu.HBM)


def project_kernel(
    rows_hbm, key_hbm, value_hbm, own_ref, to1_ref, to2_ref, to3_ref, rows_ref, weight_ref, sems
):
    copies = [
        pltpu.make_async_copy(key_hbm, weight_ref.at[:, :HD], sems.at[0]),
        pltpu.make_async_copy(value_hbm, weight_ref.at[:, HD:], sems.at[1]),
        pltpu.make_async_copy(rows_hbm, rows_ref, sems.at[2]),
    ]
    for copy in copies:
        copy.start()
    for copy in copies:
        copy.wait()
    weight = weight_ref[...]
    y = lax.axis_index("seq") // NZ
    size = own_ref.shape[0]
    for k, ref in zip((0,) + Y_STEPS, (own_ref, to1_ref, to2_ref, to3_ref)):
        first = pl.multiple_of((y ^ k) * size, size)
        ref[...] = jnp.dot(
            rows_ref[pl.ds(first, size), :], weight, preferred_element_type=jnp.float32
        ).astype(ref.dtype)


def project(rows, key_weight, value_weight):
    tokens, features = rows.shape
    return pl.pallas_call(
        project_kernel,
        in_specs=[whole(pltpu.HBM)] * 3,
        out_specs=[whole()] * NY,
        out_shape=[jax.ShapeDtypeStruct((tokens // NY, 2 * HD), jnp.float32)]
        + [jax.ShapeDtypeStruct((tokens // NY, 2 * HD), jnp.bfloat16)] * (NY - 1),
        scratch_shapes=[
            VMEM((tokens, features), jnp.bfloat16),
            VMEM((features, 2 * HD), jnp.bfloat16),
            pltpu.SemaphoreType.DMA((3,)),
        ],
        compiler_params=pltpu.CompilerParams(vmem_limit_bytes=8 * MIB),
        name="project",
    )(in_hbm(rows), in_hbm(key_weight), in_hbm(value_weight))


def fold_kernel(after_ref, own_ref, from1_ref, from2_ref, from3_ref, out_ref):
    total = own_ref[...]
    for ref in (from1_ref, from2_ref, from3_ref):
        total = total + ref[...].astype(jnp.float32)
    total = total.astype(jnp.bfloat16)
    size = total.shape[0] // NZ
    for z in range(NZ):
        place = listed(NY * NZ - NZ + z) * size
        out_ref[place : place + size, :] = total[z * size : (z + 1) * size]


def fold(after, parts):
    return pl.pallas_call(
        fold_kernel,
        in_specs=[whole()] * 5,
        out_specs=whole(),
        out_shape=jax.ShapeDtypeStruct(parts[0].shape, parts[1].dtype),
        compiler_params=pltpu.CompilerParams(vmem_limit_bytes=8 * MIB),
        name="fold",
    )(after, *parts)


def stacked_queries(query_ref, per_group):
    query = query_ref[...]
    return jnp.concatenate(
        [query[:, h * HD : (h + 1) * HD] for h in range(per_group)], axis=0
    )


def cache_kernel(
    requests,
    per_group,
    len_hbm,
    query_hbm,
    target_hbm,
    request_hbm,
    keys_hbm,
    values_hbm,
    o_ref,
    m_ref,
    l_ref,
    place_key_ref,
    place_value_ref,
    live_ref,
    stacked_ref,
    len_ref,
    query_ref,
    target_ref,
    request_ref,
    keys_ref,
    values_ref,
    query_rows,
    o_rows,
    m_rows,
    l_rows,
    small_sems,
    sems,
):
    seq_index = lax.axis_index("seq")
    rows = requests * per_group
    local_len = keys_ref.shape[1]
    tokens = live_ref.shape[1]
    small = [
        pltpu.make_async_copy(source, dest, small_sems.at[i])
        for i, (source, dest) in enumerate(
            (
                (len_hbm, len_ref),
                (query_hbm, query_ref),
                (target_hbm, target_ref),
                (request_hbm, request_ref),
            )
        )
    ]
    key_copies = [
        pltpu.make_async_copy(keys_hbm.at[r], keys_ref.at[r], sems.at[0, r])
        for r in range(requests)
    ]
    value_copies = [
        pltpu.make_async_copy(values_hbm.at[r], values_ref.at[r], sems.at[1, r])
        for r in range(requests)
    ]
    for copy in small:
        copy.start()
    for r in range(requests):
        key_copies[r].start()
        value_copies[r].start()
    for copy in small:
        copy.wait()

    per_tile = HD // tokens
    first = pl.multiple_of(seq_index // per_tile * HD, HD)
    shift = lax.rem(HD - lax.rem(seq_index, per_tile) * tokens, HD)

    def own(ref):
        tile = jnp.broadcast_to(ref[:, pl.ds(first, HD)], (8, HD))
        return pltpu.roll(tile, shift, 1)[0:1, :tokens]

    target_row = own(target_ref)
    target = jnp.broadcast_to(target_row, (tokens, tokens))
    i = lax.broadcasted_iota(jnp.int32, (tokens, tokens), 0)
    j = lax.broadcasted_iota(jnp.int32, (tokens, tokens), 1)
    column = jnp.sum(jnp.where(i == j, target, 0), axis=1, keepdims=True)
    rank = jnp.sum(jnp.where((column == target) & (i < j), 1, 0), axis=0, keepdims=True)
    slot = target_row * CAP + rank
    count = place_key_ref.shape[0]
    row = lax.broadcasted_iota(jnp.int32, (count, tokens), 0)
    dest, within = listed(row // TAIL), row % TAIL
    wanted = jnp.broadcast_to(slot, (count, tokens))
    is_key = (within < CAP) & (wanted == dest * CAP + within)
    is_value = (within >= CAP) & (within < 2 * CAP) & (wanted == dest * CAP + within - CAP)
    place_key_ref[...] = jnp.where(is_key, 1.0, 0.0).astype(jnp.bfloat16)
    place_value_ref[...] = jnp.where(is_value, 1.0, 0.0).astype(jnp.bfloat16)
    owner = jnp.broadcast_to(own(request_ref), (rows, tokens))
    mine = lax.broadcasted_iota(jnp.int32, (rows, tokens), 0) % requests
    live_ref[...] = jnp.where(owner == mine, 1.0, 0.0)

    stacked = stacked_queries(query_ref, per_group)
    stacked_ref[...] = stacked
    query_rows[...] = stacked.astype(jnp.float32)
    for r in range(requests):
        query = query_rows[pl.ds(r, per_group, stride=requests), :].astype(jnp.bfloat16)
        key_copies[r].wait()
        scores = lax.dot_general(
            query, keys_ref[r], (((1,), (1,)), ((), ())), preferred_element_type=jnp.float32
        ) * HD ** (-0.5)
        position = seq_index * local_len + lax.broadcasted_iota(jnp.int32, scores.shape, 1)
        allowed = position < len_ref[r]
        scores = jnp.where(allowed, scores, DEAD)
        top = jnp.max(scores, axis=1, keepdims=True)
        weights = jnp.where(allowed, jnp.exp(scores - top), 0.0)
        own_rows = pl.ds(r * per_group, per_group)
        l_rows[own_rows, :] = jnp.broadcast_to(
            jnp.sum(weights, axis=1, keepdims=True), (per_group, HD)
        )
        m_rows[own_rows, :] = jnp.broadcast_to(top, (per_group, HD))
        value_copies[r].wait()
        o_rows[own_rows, :] = jnp.dot(
            weights.astype(jnp.bfloat16), values_ref[r], preferred_element_type=jnp.float32
        )
    for h in range(per_group):
        to = pl.ds(h * requests, requests)
        of = pl.ds(h, requests, stride=per_group)
        o_ref[to, :] = o_rows[of, :]
        m_ref[to, :] = m_rows[of, :]
        l_ref[to, :] = l_rows[of, :]


def cache_part(cache_len, query, keys, values, target, request_ids, seq_count):
    requests, local_len, _ = keys.shape
    per_group = query.shape[1] // HD
    rows = requests * per_group
    tokens = target.shape[1] // seq_count
    f32 = jnp.float32
    table = jax.ShapeDtypeStruct((rows, HD), f32)
    place = jax.ShapeDtypeStruct((seq_count * TAIL, tokens), jnp.bfloat16)
    operands = (cache_len, query, target, request_ids, keys, values)
    return pl.pallas_call(
        functools.partial(cache_kernel, requests, per_group),
        in_specs=[whole(pltpu.HBM)] * 6,
        out_specs=[whole()] * 7,
        out_shape=[
            table,
            table,
            table,
            place,
            place,
            jax.ShapeDtypeStruct((rows, tokens), f32),
            jax.ShapeDtypeStruct((rows, HD), query.dtype),
        ],
        scratch_shapes=[SMEM(cache_len.shape, cache_len.dtype)]
        + [VMEM(a.shape, a.dtype) for a in operands[1:]]
        + [VMEM((rows, HD), f32)] * 4
        + [pltpu.SemaphoreType.DMA((4,)), pltpu.SemaphoreType.DMA((2, requests))],
        cost_estimate=pl.CostEstimate(
            flops=4 * rows * local_len * HD,
            bytes_accessed=4 * requests * local_len * HD,
            transcendentals=rows * local_len,
        ),
        compiler_params=pltpu.CompilerParams(vmem_limit_bytes=16 * MIB),
        name="cache_part",
    )(*[in_hbm(a) for a in operands])


def span_kernel(
    parts_ref,
    o_ref,
    m_ref,
    l_ref,
    place_key_ref,
    place_value_ref,
    live_ref,
    query_ref,
    out_ref,
):
    rows = o_ref.shape[0]
    seq_count = out_ref.shape[0]
    total = parts_ref[0].astype(jnp.float32)
    for source in range(1, parts_ref.shape[0]):
        total = total + parts_ref[source].astype(jnp.float32)
    owned = total.astype(jnp.bfloat16)
    span_k, span_v = owned[:, :HD], owned[:, HD:]
    live = live_ref[...] > 0.5
    scores = lax.dot_general(
        query_ref[...], span_k, (((1,), (1,)), ((), ())), preferred_element_type=jnp.float32
    ) * HD ** (-0.5)
    scores = jnp.where(live, scores, DEAD)
    m_cache = m_ref[:, 0:1]
    reference = (
        jnp.maximum(m_cache, jnp.max(scores, axis=1, keepdims=True))
        .astype(jnp.bfloat16)
        .astype(jnp.float32)
    )
    weights = jnp.where(live, jnp.exp(scores - reference), 0.0)
    scale = jnp.exp(m_cache - reference)
    row_sum = scale * l_ref[:, 0:1] + jnp.sum(weights, axis=1, keepdims=True)
    weighted = scale * o_ref[...] + jnp.dot(
        weights.astype(jnp.bfloat16), span_v, preferred_element_type=jnp.float32
    )
    empty = row_sum == 0.0
    shared = jnp.where(empty, 0.0, weighted / jnp.where(empty, 1.0, row_sum)).astype(jnp.bfloat16)
    sum_high = row_sum.astype(jnp.bfloat16).astype(jnp.float32)
    sum_low = row_sum - sum_high
    lane = lax.broadcasted_iota(jnp.int32, (rows, HD), 1)
    row = lax.broadcasted_iota(jnp.int32, (rows, HD), 0)
    spread = jnp.where(lane == row, reference, 0.0)
    spread = jnp.where(lane == row + rows, sum_high, spread)
    spread = jnp.where(lane == row + 2 * rows, sum_low, spread)
    stats = jnp.sum(spread, axis=0, keepdims=True)
    tail = jnp.dot(place_key_ref[...], span_k, preferred_element_type=jnp.float32)
    tail = tail + jnp.dot(place_value_ref[...], span_v, preferred_element_type=jnp.float32)
    within = lax.broadcasted_iota(jnp.int32, tail.shape, 0) % TAIL
    tail = jnp.where(within == 2 * CAP, jnp.broadcast_to(stats, tail.shape), tail)
    out_ref[:, rows:, :] = tail.astype(jnp.bfloat16).reshape(seq_count, TAIL, HD)
    for dest in range(seq_count):
        out_ref[dest, :rows, :] = shared


def span_part(parts, cache_state, seq_count):
    rows = cache_state[0].shape[0]
    return pl.pallas_call(
        span_kernel,
        in_specs=[whole()] * (1 + len(cache_state)),
        out_specs=whole(),
        out_shape=jax.ShapeDtypeStruct((seq_count, rows + TAIL, HD), jnp.bfloat16),
        compiler_params=pltpu.CompilerParams(vmem_limit_bytes=8 * MIB),
        name="span_part",
    )(parts, *cache_state)


def out_kernel(requests, message_ref, weight_ref, out_ref):
    seq_count = message_ref.shape[0]
    rows = message_ref.shape[1] - TAIL
    per_group = rows // requests
    tails = message_ref[:, rows:, :].astype(jnp.float32)
    within = lax.broadcasted_iota(jnp.int32, tails.shape, 1)
    stats = jnp.sum(jnp.where(within == 2 * CAP, tails, 0.0), axis=1)
    m = stats[:, :rows]
    sums = stats[:, rows : 2 * rows] + stats[:, 2 * rows : 3 * rows]
    share = jnp.exp(m - jnp.max(m, axis=0, keepdims=True)) * sums
    share = share / jnp.sum(share, axis=0, keepdims=True)
    share = share.T
    total = jnp.zeros((rows, HD), jnp.float32)
    for source in range(seq_count):
        total = total + share[:, source : source + 1] * message_ref[source, :rows, :].astype(
            jnp.float32
        )
    attended = jnp.concatenate(
        [total[h * requests : (h + 1) * requests] for h in range(per_group)], axis=1
    ).astype(jnp.bfloat16)
    projected = jnp.dot(attended, weight_ref[...], preferred_element_type=jnp.float32)
    for dest in range(out_ref.shape[0]):
        out_ref[dest] = projected


def out_part(messages, out_weight, requests, tp_count):
    return pl.pallas_call(
        functools.partial(out_kernel, requests),
        in_specs=[whole()] * 2,
        out_specs=whole(),
        out_shape=jax.ShapeDtypeStruct((tp_count, requests, out_weight.shape[1]), jnp.float32),
        compiler_params=pltpu.CompilerParams(vmem_limit_bytes=8 * MIB),
        name="out_part",
    )(messages, out_weight)


def finish_kernel(
    message_ref, share_ref, out_hbm, key_hbm, value_hbm, out_ref, key_ref, value_ref, sems
):
    rows = message_ref.shape[1] - TAIL
    tails = message_ref[:, rows:, :]
    count = tails.shape[0]
    tails = jnp.concatenate(
        [tails[p : p + 1] for p in (listed(seq) for seq in range(count))], axis=0
    )
    key_ref[...] = tails[:, :CAP].reshape(key_ref.shape)
    value_ref[...] = tails[:, CAP : 2 * CAP].reshape(value_ref.shape)
    copies = [
        pltpu.make_async_copy(source, dest, sems.at[i])
        for i, (source, dest) in enumerate(
            ((out_ref, out_hbm), (key_ref, key_hbm), (value_ref, value_hbm))
        )
    ]
    copies[1].start()
    copies[2].start()
    out_ref[...] = jnp.sum(share_ref[...], axis=0).astype(jnp.bfloat16)
    copies[0].start()
    for copy in copies:
        copy.wait()


def finish(messages, shares):
    slots = jax.ShapeDtypeStruct((messages.shape[0] * CAP, HD), jnp.bfloat16)
    outs = [jax.ShapeDtypeStruct(shares.shape[1:], jnp.bfloat16), slots, slots]
    return pl.pallas_call(
        finish_kernel,
        in_specs=[whole()] * 2,
        out_specs=[whole(pltpu.HBM)] * 3,
        out_shape=outs,
        scratch_shapes=[VMEM(a.shape, a.dtype) for a in outs] + [pltpu.SemaphoreType.DMA((3,))],
        compiler_params=pltpu.CompilerParams(vmem_limit_bytes=8 * MIB),
        name="finish",
    )(messages, shares)


def per_device(
    decode_query,
    cache_keys,
    cache_values,
    cache_len,
    prefill_rows,
    key_weight,
    value_weight,
    span_request,
    span_target,
    out_weight,
):
    seq_count = lax.axis_size("seq")
    tp_count = lax.axis_size("tp")
    requests = cache_keys.shape[0]
    rows = requests * decode_query.shape[1] // HD
    pre_dev = prefill_rows.shape[0] // seq_count

    own, *sent = project(prefill_rows, key_weight, value_weight)
    seq = [(y, z) for y in range(NY) for z in range(NZ)]
    came = [
        lax.ppermute(part, "seq", [(y * NZ + z, (y ^ k) * NZ + z) for y, z in seq])
        for k, part in zip(Y_STEPS, sent)
    ]
    targets = span_target.T
    request_ids = span_request.reshape(targets.shape)
    cache_state = cache_part(
        cache_len, decode_query, cache_keys, cache_values, targets, request_ids, seq_count
    )
    z_order = [listed(NY * NZ - NZ + place) for place in range(NZ)]
    partial = fold(cache_state[0], [own, *came]).reshape(NZ, pre_dev, 2 * HD)
    parts = lax.all_to_all(
        partial,
        "seq",
        split_axis=0,
        concat_axis=0,
        tiled=True,
        axis_index_groups=[[y * NZ + z for z in z_order] for y in range(NY)],
    )
    outgoing = span_part(parts, cache_state, seq_count)
    messages = lax.all_to_all(
        outgoing,
        "seq",
        split_axis=0,
        concat_axis=0,
        tiled=True,
        axis_index_groups=[[listed(place) for place in range(seq_count)]],
    )
    shares = out_part(messages, out_weight, requests, tp_count)
    shares = lax.all_to_all(
        shares,
        "tp",
        split_axis=0,
        concat_axis=0,
        tiled=True,
        axis_index_groups=[[listed(NY * NZ - NZ + place) for place in range(tp_count)]],
    )
    return finish(messages, shares)


def solution(mesh):
    placed = (
        P(None, "tp"),
        P(None, "seq", "tp"),
        P(None, "seq", "tp"),
        P(),
        P(None, "seq"),
        P("seq", "tp"),
        P("seq", "tp"),
        P(),
        P(),
        P("tp", "seq"),
    )
    return jax.shard_map(
        per_device,
        mesh=mesh,
        in_specs=placed,
        out_specs=(P(None, "seq"), P("seq", "tp"), P("seq", "tp")),
        check_vma=False,
    )
```
